32 devices in a mesh: dp: 8 (over y, x, core), mp: 4 (over z).
Axes of the slice: x: 2, y: 2, z: 4, core: 2. Of those that a mesh axis runs over, the one named last changes fastest.
Arguments:
- patches: bfloat16 [256, 81920], P('dp', 'mp'), may hold values from -10 to 10
- norm_gain: float32 [1280], replicated, may hold values from 0.1 to 1.9
- qkv_weight: bfloat16 [1280, 3840], P(None, 'mp'), may hold values from -6 to 6
- out_weight: bfloat16 [1280, 1280], P('mp'), may hold values from -0.15625 to 0.15625
- window_plan: int32 [8, 32], replicated, may hold values from -1 to 7, as said below
Outputs:
- attended: bfloat16 [256, 81920], P('dp', 'mp')
The draws below stay inside these ranges and needn't reach their ends.
Inputs may be any that keep to these rules, and one draw needn't show every extreme that they name: `window_plan`: each home's live slots come first; over all homes every encoder device is named by exactly 16 slots; one home names one encoder at most 4 times and some home reaches that; the busiest home has all 32 slots live.
All inputs are finite; a program needn't handle non-finite values.
Results may differ from the reference program's by a relative error of at most 0.018.
Values may be sent and summed in bfloat16 or wider, within the bound.
A program may use at most 128 MiB of HBM per device.

```python
import math
import jax
import jax.numpy as jnp
from jax import lax

D = 1280
HEADS = 16
HEAD_DIM = 80
WIN = 64
ENC_WIN = 16
HOME_WIN = 32
HOMES = 8
WINDOWS = 256
ROWS = 16384
N_MP = 4


def draw_patches(key, part):
    first_key, second_key, third_key = jax.random.split(jax.random.fold_in(key, 11), 3)
    draws_raw = jnp.clip(jax.random.normal(first_key, (ROWS, D), jnp.float32), -3.0, 3.0)
    row_scale = jnp.exp(jax.random.uniform(second_key, (ROWS, 1), jnp.float32, math.log(0.1), math.log(1.0)))
    col_scale = jnp.exp(jax.random.uniform(third_key, (1, D), jnp.float32, math.log(0.25), math.log(2.5)))
    values = (draws_raw * row_scale * col_scale).reshape(ROWS // WIN, WIN, D)
    return jnp.transpose(values, (0, 2, 1)).reshape(ROWS // WIN, D * WIN).astype(jnp.bfloat16)


def draw_qkv_weight(key, part):
    first_key = jax.random.fold_in(jax.random.fold_in(key, 23), 0)
    weights = jnp.clip(jax.random.normal(first_key, (D, HEADS, 3, HEAD_DIM), jnp.float32), -4.0, 4.0) * D ** (-0.5)
    return weights.reshape(D, 3 * D).astype(jnp.bfloat16)


def draw_window_plan(key, part):
    first_key, second_key, third_key = jax.random.split(jax.random.fold_in(key, 37), 3)
    home_order = jax.random.permutation(first_key, HOMES)
    spread = jax.random.randint(second_key, (HOMES // 2,), 0, ENC_WIN + 1).astype(jnp.int32)
    spread = spread.at[0].set(ENC_WIN)
    paired = jnp.stack([ENC_WIN + spread, ENC_WIN - spread], axis=1).reshape(HOMES)
    counts = jnp.zeros((HOMES,), jnp.int32).at[home_order].set(paired)
    offsets = jnp.cumsum(counts) - counts
    targets = jax.random.permutation(third_key, HOMES).astype(jnp.int32)
    columns = jnp.arange(HOME_WIN, dtype=jnp.int32)
    encoder_of = targets[(offsets[:, None] + columns[None, :]) % HOMES]
    return jnp.where(columns[None, :] < counts[:, None], encoder_of, -1).astype(jnp.int32)


def levels(own_key, extent, cuts, least, largest):
    def one(axis_at, shards_of):
        steps = jax.random.uniform(jax.random.fold_in(jax.random.fold_in(own_key, 6), axis_at), (shards_of,), jnp.float32, least / len(cuts), largest / len(cuts))
        return jnp.repeat(jnp.exp(steps), extent[axis_at] // shards_of).reshape((-1,) + (1,) * (len(extent) - axis_at - 1))

    gain = one(*cuts[0])
    for cut in cuts[1:]:
        gain = gain * one(*cut)
    return gain


def noise(key, dims, deviation, bound, shards=(), kind=jnp.bfloat16):
    array = jax.random.normal(key, dims, jnp.float32) * deviation
    if len(shards) > 0:
        array = levels(key, dims, shards, -0.22, 0.18) * array
    return jnp.clip(array, min=-bound, max=bound).astype(kind)


def setup_inputs(seed: int = 0) -> dict:
    key_of = jax.random.split(jax.random.key(seed), 6)
    patches = draw_patches(jax.random.fold_in(key_of[5], 71), 0)
    norm_gain = jnp.clip(1.0 + 0.18 * jax.random.normal(key_of[1], (D,), jnp.float32), 0.1, 1.9)
    qkv_weight = draw_qkv_weight(jax.random.fold_in(key_of[5], 71), 0)
    out_weight = noise(key_of[3], (D, D), D ** -0.5, 0.15625, ((0, 4),))
    window_plan = draw_window_plan(jax.random.fold_in(key_of[5], 71), 0)
    return dict(patches=patches, norm_gain=norm_gain, qkv_weight=qkv_weight, out_weight=out_weight, window_plan=window_plan)


epsilon = 1e-06

def attend(window_block, norm_gain, qkv_weight, out_weight):
    count = window_block.shape[0]
    as_float = window_block.astype(jnp.float32)
    mean_square = lax.optimization_barrier(jnp.mean(as_float * as_float, axis=-1, keepdims=True))
    normed = (as_float * lax.rsqrt(mean_square + epsilon) * norm_gain).astype(jnp.bfloat16)
    projected = jnp.dot(normed.reshape(count * WIN, D), qkv_weight, preferred_element_type=jnp.float32)
    projected = lax.optimization_barrier(projected.astype(jnp.bfloat16)).astype(jnp.float32)
    projected = projected.reshape(count, WIN, HEADS, 3, HEAD_DIM)
    queries = projected[:, :, :, 0, :]
    key_vecs = projected[:, :, :, 1, :]
    value_vecs = projected[:, :, :, 2, :]
    scores = jnp.einsum('wqhd,wkhd->whqk', queries, key_vecs) * HEAD_DIM ** (-0.5)
    probs = jax.nn.softmax(scores, axis=-1)
    probs = lax.optimization_barrier(probs.astype(jnp.bfloat16)).astype(jnp.float32)
    heads_out = jnp.einsum('whqk,wkhd->wqhd', probs, value_vecs).astype(jnp.bfloat16)
    flat_heads = heads_out.reshape(count * WIN, D)
    group_width = D // N_MP
    summed = jnp.zeros((count * WIN, D), jnp.float32)
    for group in range(N_MP):
        lower = group * group_width
        piece = flat_heads[:, lower:lower + group_width]
        partial_term = jnp.dot(piece, out_weight[lower:lower + group_width, :], preferred_element_type=jnp.float32)
        partial_term = lax.optimization_barrier(partial_term.astype(jnp.bfloat16)).astype(jnp.float32)
        summed = summed + partial_term
    block_out = (as_float + summed.reshape(count, WIN, D)).astype(jnp.bfloat16)
    return block_out

def reference(patches, norm_gain, qkv_weight, out_weight, window_plan):
    blocks = jnp.transpose(patches.reshape(WINDOWS, D, WIN), (0, 2, 1)).reshape(HOMES, HOME_WIN, WIN, D)
    results = lax.map(lambda window_block: attend(window_block, norm_gain, qkv_weight, out_weight), blocks)
    live_mask = (window_plan >= 0)[:, :, None, None]
    results = jnp.where(live_mask, results, jnp.zeros_like(results))
    results = jnp.transpose(results.reshape(WINDOWS, WIN, D), (0, 2, 1))
    return results.reshape(WINDOWS, D * WIN)
```

```python
import functools

import jax
import jax.numpy as jnp
from jax import lax
from jax.experimental import pallas as pl
from jax.experimental.pallas import tpu as pltpu
from jax.sharding import PartitionSpec as P

HEAD_DIM = 80
WIN = 64
ENC_WIN = 16
LANES = 128
PAIRS = 2

epsilon = 1e-06
MESH = pl.DeviceIdType.MESH
F32 = jnp.float32
BF16 = jnp.bfloat16


def kernel(
    n, m, cap,
    source_ref, chosen_ref, back_ref, slot_ref, x_ref, gain_ref, qkv_ref, outw_ref,
    out_ref,
    outb, inb, gath, qkv_t, outw_t, proj, heads, part, from_left, from_right, total, done, backb, homeb,
    d_send, d_recv, b_send, b_recv, ag_recv, ag_right, ag_left, rs_send, rs_left, rs_right,
):
    me = lax.axis_index("dp")
    z = lax.axis_index("mp")
    home_win, rows, _ = x_ref.shape
    width = 2 * rows
    chunks = gath.shape[1]
    heads_here = qkv_ref.shape[1] // (3 * HEAD_DIM)

    barrier = pltpu.get_barrier_semaphore()

    def greet(d, _):
        pl.semaphore_signal(
            barrier, inc=1, device_id={"dp": lax.rem(me + d, n)}, device_id_type=MESH
        )
        return 0

    lax.fori_loop(1, n, greet, 0)

    @pl.when(z > 0)
    def _():
        pl.semaphore_signal(barrier, inc=1, device_id={"mp": z - 1}, device_id_type=MESH)

    @pl.when(z < m - 1)
    def _():
        pl.semaphore_signal(barrier, inc=1, device_id={"mp": z + 1}, device_id_type=MESH)

    def pack(d, _):
        e = lax.rem(me + d, n)
        for j in range(cap):
            outb[e, j] = x_ref[source_ref[e * cap + j]]
        return 0

    lax.fori_loop(0, n, pack, 0)
    ends = (z == 0).astype(jnp.int32) + (z == m - 1).astype(jnp.int32)
    pl.semaphore_wait(barrier, n + 1 - ends)

    def exchange(src, dst, send, recv, d):
        e = lax.rem(me + d, n)
        return pltpu.make_async_remote_copy(
            src_ref=src.at[e], dst_ref=dst.at[me], send_sem=send.at[d], recv_sem=recv.at[d],
            device_id={"dp": e}, device_id_type=MESH,
        )

    def start_exchange(src, dst, send, recv):
        def step(d, _):
            exchange(src, dst, send, recv, d).start()
            return 0

        lax.fori_loop(1, n, step, 0)

    def end_exchange(src, dst, send, recv):
        def step(d, _):
            exchange(src, dst, send, recv, d).wait()
            return 0

        lax.fori_loop(1, n, step, 0)

    start_exchange(outb, inb, d_send, d_recv)
    inb[me] = outb[me]

    lower = 0
    while lower < qkv_ref.shape[1]:
        size = min(LANES, qkv_ref.shape[1] - lower)
        qkv_t[lower:lower + size, :] = qkv_ref[:, lower:lower + size].T
        lower += size
    for lower in range(0, outw_ref.shape[1], LANES):
        outw_t[lower:lower + LANES, :] = outw_ref[:, lower:lower + LANES].T

    row = lax.broadcasted_iota(jnp.int32, (width, width), 0)
    col = lax.broadcasted_iota(jnp.int32, (width, width), 1)
    spread = jnp.where(
        row == jnp.where(col < rows, 2 * col, 2 * (col - rows) + 1), 1.0, 0.0
    ).astype(BF16)
    gathered = jnp.where(
        col == jnp.where(row < rows, 2 * row, 2 * (row - rows) + 1), 1.0, 0.0
    ).astype(BF16)
    low_half = lax.broadcasted_iota(jnp.int32, (rows, LANES), 1) < WIN

    end_exchange(outb, inb, d_send, d_recv)

    def window_in(k):
        at = chosen_ref[k]
        return inb[at // cap, lax.rem(at, cap)].astype(F32)

    def unpack(c, _):
        for p in range(PAIRS):
            first = window_in((c * PAIRS + p) * 2)
            second = window_in((c * PAIRS + p) * 2 + 1)
            even = jnp.where(low_half, first, pltpu.roll(second, WIN, 1))
            odd = jnp.where(low_half, pltpu.roll(first, WIN, 1), second)
            halves = jnp.concatenate([even, odd], axis=0).astype(BF16)
            block = jnp.dot(spread, halves, preferred_element_type=F32).astype(BF16)
            gath[z, c, :, p * LANES:(p + 1) * LANES] = block
        return 0

    def ag_copy(c, o, step, send):
        return pltpu.make_async_remote_copy(
            src_ref=gath.at[o, c], dst_ref=gath.at[o, c],
            send_sem=send.at[c, o], recv_sem=ag_recv.at[c, o],
            device_id={"mp": z + step}, device_id_type=MESH,
        )

    def ag_own(c):
        @pl.when(z < m - 1)
        def _():
            ag_copy(c, z, 1, ag_right).start()

        @pl.when(z > 0)
        def _():
            ag_copy(c, z, -1, ag_left).start()

    def ag_step(c, t):
        @pl.when(z >= t)
        def _():
            ag_copy(c, z - t, -1, ag_left).wait_recv()

            @pl.when(z < m - 1)
            def _():
                ag_copy(c, z - t, 1, ag_right).start()

        @pl.when(z + t < m)
        def _():
            ag_copy(c, z + t, 1, ag_right).wait_recv()

            @pl.when(z > 0)
            def _():
                ag_copy(c, z + t, -1, ag_left).start()

    def rs_copy(c, s, step, landing, recv):
        return pltpu.make_async_remote_copy(
            src_ref=part.at[c, s], dst_ref=landing.at[c, s],
            send_sem=rs_send.at[c, s], recv_sem=recv.at[c, s],
            device_id={"mp": z + step}, device_id_type=MESH,
        )

    def rs_stage(c, k):
        @pl.when(z == k)
        def _():
            def step(i, _):
                s = m - 1 - i
                if k > 0:
                    rs_copy(c, s, -1, from_left, rs_left).wait_recv()
                    part[c, s] = (part[c, s].astype(F32) + from_left[c, s].astype(F32)).astype(BF16)
                rs_copy(c, s, 1, from_left, rs_left).start()
                return 0

            lax.fori_loop(0, m - 1 - k, step, 0)

        @pl.when(z == m - 1 - k)
        def _():
            def step(s, _):
                if k > 0:
                    rs_copy(c, s, 1, from_right, rs_right).wait_recv()
                    part[c, s] = (part[c, s].astype(F32) + from_right[c, s].astype(F32)).astype(BF16)
                rs_copy(c, s, -1, from_right, rs_right).start()
                return 0

            lax.fori_loop(0, m - 1 - k, step, 0)

    def rs_final(c):
        total[...] = part[c, z].astype(F32)

        @pl.when(z > 0)
        def _():
            rs_copy(c, z, -1, from_left, rs_left).wait_recv()
            total[...] += from_left[c, z].astype(F32)

        @pl.when(z < m - 1)
        def _():
            rs_copy(c, z, 1, from_right, rs_right).wait_recv()
            total[...] += from_right[c, z].astype(F32)

        block = (total[...] + gath[z, c].astype(F32)).astype(BF16)
        halves = jnp.dot(gathered, block, preferred_element_type=F32)
        for p in range(PAIRS):
            even = halves[:rows, p * LANES:(p + 1) * LANES]
            odd = halves[rows:, p * LANES:(p + 1) * LANES]
            k = (c * PAIRS + p) * 2
            done[k] = jnp.where(low_half, even, pltpu.roll(odd, WIN, 1)).astype(BF16)
            done[k + 1] = jnp.where(low_half, pltpu.roll(even, WIN, 1), odd).astype(BF16)

    def project(c):
        full = gath[:, c].reshape(m * width, PAIRS * LANES).astype(F32)
        mean_square = jnp.mean(full * full, axis=0, keepdims=True)
        normed = (full * lax.rsqrt(mean_square + epsilon) * gain_ref[...]).astype(BF16)
        proj[...] = jnp.dot(qkv_t[...], normed, preferred_element_type=F32).astype(BF16)

    key_window = lax.broadcasted_iota(jnp.int32, (LANES, LANES), 0) // WIN
    query_window = lax.broadcasted_iota(jnp.int32, (LANES, LANES), 1) // WIN
    same_window = key_window == query_window

    def attend(p):
        lanes = slice(p * LANES, (p + 1) * LANES)
        for h in range(heads_here):
            base = h * 3 * HEAD_DIM
            queries = proj[base:base + HEAD_DIM, lanes]
            key_vecs = proj[base + HEAD_DIM:base + 2 * HEAD_DIM, lanes]
            value_vecs = proj[base + 2 * HEAD_DIM:base + 3 * HEAD_DIM, lanes]
            scores = lax.dot_general(
                key_vecs, queries, (((0,), (0,)), ((), ())), preferred_element_type=F32
            ) * HEAD_DIM ** (-0.5)
            scores = jnp.where(same_window, scores, -1e30)
            weights = jnp.exp(scores - jnp.max(scores, axis=0, keepdims=True))
            probs = (weights / jnp.sum(weights, axis=0, keepdims=True)).astype(BF16)
            heads[h * HEAD_DIM:(h + 1) * HEAD_DIM, lanes] = jnp.dot(
                value_vecs, probs, preferred_element_type=F32
            ).astype(BF16)

    def output(c):
        for s in range(m):
            part[c, s] = jnp.dot(
                outw_t[s * width:(s + 1) * width, :], heads[...], preferred_element_type=F32
            ).astype(BF16)

    lax.fori_loop(0, chunks, unpack, 0)
    ag_own(0)
    if chunks > 1:
        ag_own(1)
    for t in range(1, m):
        ag_step(0, t)

    between = PAIRS + 1

    def steps_at(place):
        return [t for t in range(1, m) if (t - 1) * between // (m - 1) == place]

    def turn(c, _):
        @pl.when(c + 2 < chunks)
        def _():
            ag_own(c + 2)

        for place in range(between):
            @pl.when(c < chunks)
            def _():
                if place == 0:
                    project(c)
                else:
                    attend(place - 1)

            @pl.when(c + 1 < chunks)
            def _():
                for t in steps_at(place):
                    ag_step(c + 1, t)

            @pl.when(c > 0)
            def _():
                for t in steps_at(place):
                    if t < m - 1:
                        rs_stage(c - 1, t)
                    else:
                        rs_final(c - 1)

        @pl.when(c < chunks)
        def _():
            output(c)
            rs_stage(c, 0)

        return 0

    lax.fori_loop(0, chunks + 1, turn, 0)

    def reply(d, _):
        e = lax.rem(me + d, n)
        for j in range(cap):
            backb[e, j] = done[back_ref[e * cap + j]]
        return 0

    lax.fori_loop(0, n, reply, 0)
    start_exchange(backb, homeb, b_send, b_recv)
    homeb[me] = backb[me]

    def sent(c, _):
        def each(o, _):
            @pl.when(jnp.logical_and(z < m - 1, o <= z))
            def _():
                ag_copy(c, o, 1, ag_right).wait_send()

            @pl.when(jnp.logical_and(z > 0, o >= z))
            def _():
                ag_copy(c, o, -1, ag_left).wait_send()

            @pl.when(o > z)
            def _():
                rs_copy(c, o, 1, from_left, rs_left).wait_send()

            @pl.when(o < z)
            def _():
                rs_copy(c, o, -1, from_right, rs_right).wait_send()

            return 0

        return lax.fori_loop(0, m, each, 0)

    lax.fori_loop(0, chunks, sent, 0)
    end_exchange(backb, homeb, b_send, b_recv)

    def place_home(s, _):
        at = slot_ref[s]
        safe = jnp.maximum(at, 0)
        found = homeb[safe // cap, lax.rem(safe, cap)].astype(F32)
        out_ref[s] = jnp.where(at >= 0, found, jnp.zeros_like(found)).astype(BF16)
        return 0

    lax.fori_loop(0, home_win, place_home, 0)


def body(patches, norm_gain, qkv_weight, out_weight, window_plan):
    n = lax.axis_size("dp")
    m = lax.axis_size("mp")
    here = lax.axis_index("dp")
    home_win, row_width = patches.shape
    rows = row_width // LANES
    width = 2 * rows
    full_width = width * m
    cap = (home_win + n - 1) // n
    chunks = ENC_WIN // (2 * PAIRS)
    cols = PAIRS * LANES

    my_plan = lax.dynamic_slice_in_dim(window_plan, here, 1, 0)[0]
    slots = jnp.arange(home_win, dtype=jnp.int32)
    earlier = (my_plan[:, None] == my_plan[None, :]) & (slots[None, :] < slots[:, None])
    ordinal = jnp.sum(earlier.astype(jnp.int32), axis=1)
    slot_index = jnp.where(my_plan >= 0, my_plan * cap + ordinal, -1)
    all_slots = jnp.arange(n * cap, dtype=jnp.int32)
    source = jnp.sum(
        jnp.where(slot_index[None, :] == all_slots[:, None], slots[None, :], 0), axis=1
    )
    sent_here = jnp.sum((window_plan == here).astype(jnp.int32), axis=1)
    homes = jnp.arange(n, dtype=jnp.int32)
    offsets = jnp.sum(
        jnp.where(homes[None, :] < homes[:, None], sent_here[None, :], 0), axis=1
    )
    columns = jnp.arange(cap, dtype=jnp.int32)
    position = jnp.where(
        columns[None, :] < sent_here[:, None], offsets[:, None] + columns[None, :], -1
    ).reshape(n * cap)
    picked = position[None, :] == jnp.arange(ENC_WIN, dtype=jnp.int32)[:, None]
    chosen = jnp.sum(jnp.where(picked, all_slots[None, :], 0), axis=1)
    back = jnp.maximum(position, 0)

    smem = pl.BlockSpec(memory_space=pltpu.SMEM)
    vmem = pl.BlockSpec(memory_space=pltpu.VMEM)
    dma = pltpu.SemaphoreType.DMA
    result = pl.pallas_call(
        functools.partial(kernel, n, m, cap),
        out_shape=jax.ShapeDtypeStruct((home_win, rows, LANES), BF16),
        in_specs=[smem] * 4 + [vmem] * 4,
        out_specs=vmem,
        scratch_shapes=[
            pltpu.VMEM((n, cap, rows, LANES), BF16),
            pltpu.VMEM((n, cap, rows, LANES), BF16),
            pltpu.VMEM((m, chunks, width, cols), BF16),
            pltpu.VMEM((qkv_weight.shape[1], full_width), BF16),
            pltpu.VMEM((full_width, out_weight.shape[0]), BF16),
            pltpu.VMEM((qkv_weight.shape[1], cols), BF16),
            pltpu.VMEM((out_weight.shape[0], cols), BF16),
            pltpu.VMEM((chunks, m, width, cols), BF16),
            pltpu.VMEM((chunks, m, width, cols), BF16),
            pltpu.VMEM((chunks, m, width, cols), BF16),
            pltpu.VMEM((width, cols), F32),
            pltpu.VMEM((ENC_WIN, rows, LANES), BF16),
            pltpu.VMEM((n, cap, rows, LANES), BF16),
            pltpu.VMEM((n, cap, rows, LANES), BF16),
            dma((n,)), dma((n,)), dma((n,)), dma((n,)),
            dma((chunks, m)), dma((chunks, m)), dma((chunks, m)),
            dma((chunks, m)), dma((chunks, m)), dma((chunks, m)),
        ],
        compiler_params=pltpu.CompilerParams(
            collective_id=0, has_side_effects=True, vmem_limit_bytes=56 * 1024 * 1024
        ),
    )(
        source, chosen, back, slot_index,
        patches.reshape(home_win, rows, LANES), norm_gain[:, None], qkv_weight, out_weight,
    )
    return result.reshape(home_win, row_width)


def solution(mesh):
    return jax.shard_map(
        body,
        mesh=mesh,
        in_specs=(P("dp", "mp"), P(), P(None, "mp"), P("mp", None), P()),
        out_specs=P("dp", "mp"),
        check_vma=False,
    )
```

```python
import functools

import jax
import jax.numpy as jnp
from jax import lax
from jax.experimental import pallas as pl
from jax.experimental.pallas import tpu as pltpu
from jax.sharding import PartitionSpec as P

HEAD_DIM = 80
WIN = 64
ENC_WIN = 16
LANES = 128
PAIRS = 1

epsilon = 1e-06
MESH = pl.DeviceIdType.MESH
F32 = jnp.float32
BF16 = jnp.bfloat16


SOURCE, CHOSEN, BACK, SLOT = range(4)


def early_positions(n, cap):
    return n - (ENC_WIN - 2 * PAIRS) // cap


def position_order(n, cap):
    far = list(range(n - 1, 1, -1))
    split = early_positions(n, cap) - 3
    return far[:split] + [1, 0] + far[split:]


def position_of(flip, n, cap):
    split = early_positions(n, cap) - 3
    at = n - 1 - flip
    at = jnp.where(at >= split, at + 2, at)
    return jnp.where(flip == 1, split, jnp.where(flip == 0, split + 1, at))


def partner(me, flip):
    other, bit = me, 1
    while bit <= flip:
        if (flip // bit) % 2:
            other = other + bit * (1 - 2 * ((me // bit) % 2))
        bit *= 2
    return other


def iota(shape, axis):
    return lax.broadcasted_iota(jnp.int32, shape, axis)


def plan_indices(n, cap, me, plan_ref, index_v):
    plan = plan_ref[...]
    index_v[...] = jnp.zeros_like(index_v)
    slots = plan.shape[1]
    mine = plan_ref[pl.ds(me, 1), :]
    same = iota((slots, slots), 0) == iota((slots, slots), 1)
    turned = jnp.sum(jnp.where(same, mine, 0), axis=1, keepdims=True)
    earlier = (turned == mine) & (iota((slots, slots), 1) < iota((slots, slots), 0))
    ordinal = jnp.sum(earlier.astype(jnp.int32), axis=1, keepdims=True)
    place = jnp.where(turned >= 0, position_of(turned ^ me, n, cap) * cap + ordinal, -1)
    grid = (slots, n * cap)
    source = jnp.sum(
        jnp.where(place == iota(grid, 1), iota(grid, 0), 0), axis=0, keepdims=True
    )
    index_v[SOURCE:SOURCE + 1, :n * cap] = jnp.clip(source, 0, slots - 1)
    index_v[SLOT:SLOT + 1, :slots] = jnp.minimum(
        jnp.sum(jnp.where(same, place, 0), axis=0, keepdims=True), n * cap - 1
    )

    counts = jnp.sum((plan == me).astype(jnp.int32), axis=1, keepdims=True)
    square = (n, n)
    counts_row = jnp.sum(
        jnp.where(iota(square, 0) == iota(square, 1), counts, 0), axis=0, keepdims=True
    )
    at_col = position_of(iota((n, 1), 0) ^ me, n, cap)
    at_row = position_of(iota((1, n), 1) ^ me, n, cap)
    offsets = jnp.sum(jnp.where(at_row < at_col, counts_row, 0), axis=1, keepdims=True)
    j = iota((n, ENC_WIN), 1) - offsets
    chosen = jnp.sum(
        jnp.where((j >= 0) & (j < counts), at_col * cap + j, 0), axis=0, keepdims=True
    )
    index_v[CHOSEN:CHOSEN + 1, :ENC_WIN] = jnp.clip(chosen, 0, n * cap - 1)
    q = iota((n, n * cap), 1)
    back = jnp.sum(
        jnp.where(q // cap == at_col, offsets + q % cap, 0), axis=0, keepdims=True
    )
    index_v[BACK:BACK + 1, :n * cap] = jnp.clip(back, 0, ENC_WIN - 1)


def kernel(
    n, m, cap,
    plan_ref, x_ref, gain_ref, qkv_ref, outw_ref,
    out_ref,
    index_v, index_s, outw, gain_t, outb, inb, gath, qkv_t, outw_t, proj, heads, part, from_left, from_right, total, done, backb, homeb,
    i_sem, w_sem, d_send, d_recv, b_send, b_recv, ag_recv, ag_right, ag_left, rs_send, rs_left, rs_right,
):
    me = lax.axis_index("dp")
    z = lax.axis_index("mp")
    home_win, rows, _ = x_ref.shape
    width = 2 * rows
    chunks = gath.shape[1]
    heads_here = qkv_ref.shape[0] // (3 * HEAD_DIM)

    order = position_order(n, cap)

    load_qkv = pltpu.make_async_copy(qkv_ref, qkv_t, w_sem.at[0])
    load_outw = pltpu.make_async_copy(outw_ref, outw, w_sem.at[1])
    load_qkv.start()
    load_outw.start()

    barrier = pltpu.get_barrier_semaphore()

    for d in range(1, n):
        pl.semaphore_signal(
            barrier, inc=1, device_id={"dp": partner(me, d)}, device_id_type=MESH
        )

    @pl.when(z > 0)
    def _():
        pl.semaphore_signal(barrier, inc=1, device_id={"mp": z - 1}, device_id_type=MESH)

    @pl.when(z < m - 1)
    def _():
        pl.semaphore_signal(barrier, inc=1, device_id={"mp": z + 1}, device_id_type=MESH)

    plan_indices(n, cap, me, plan_ref, index_v)
    load_index = pltpu.make_async_copy(index_v, index_s, i_sem)
    load_index.start()
    load_index.wait()
    for p in range(n):
        for j in range(cap):
            outb[p, j] = x_ref[index_s[SOURCE, p * cap + j]]

    ends = (z == 0).astype(jnp.int32) + (z == m - 1).astype(jnp.int32)
    pl.semaphore_wait(barrier, n + 1 - ends)

    own = order.index(0)

    def exchange(src, dst, send, recv, p):
        return pltpu.make_async_remote_copy(
            src_ref=src.at[p], dst_ref=dst.at[p], send_sem=send.at[p], recv_sem=recv.at[p],
            device_id={"dp": partner(me, order[p])}, device_id_type=MESH,
        )

    others = [p for p in range(n) if p != own]
    for p in others:
        exchange(outb, inb, d_send, d_recv, p).start()
    inb[own] = outb[own]

    load_outw.wait()
    for lower in range(0, outw.shape[1], LANES):
        outw_t[lower:lower + LANES, :] = outw[:, lower:lower + LANES].T
        gain_t[lower:lower + LANES, :] = jnp.broadcast_to(
            gain_ref[:, lower:lower + LANES], (LANES, LANES)
        ).T

    row = lax.broadcasted_iota(jnp.int32, (width, width), 0)
    col = lax.broadcasted_iota(jnp.int32, (width, width), 1)
    spread = jnp.where(
        row == jnp.where(col < rows, 2 * col, 2 * (col - rows) + 1), 1.0, 0.0
    ).astype(BF16)
    gathered = jnp.where(
        col == jnp.where(row < rows, 2 * row, 2 * (row - rows) + 1), 1.0, 0.0
    ).astype(BF16)
    low_half = lax.broadcasted_iota(jnp.int32, (rows, LANES), 1) < WIN

    for p in others:
        exchange(outb, inb, d_send, d_recv, p).wait()
    load_qkv.wait()

    def window_in(k):
        at = index_s[CHOSEN, k]
        return inb[at // cap, lax.rem(at, cap)].astype(F32)

    def unpack(c, _):
        for p in range(PAIRS):
            first = window_in((c * PAIRS + p) * 2)
            second = window_in((c * PAIRS + p) * 2 + 1)
            even = jnp.where(low_half, first, pltpu.roll(second, WIN, 1))
            odd = jnp.where(low_half, pltpu.roll(first, WIN, 1), second)
            halves = jnp.concatenate([even, odd], axis=0).astype(BF16)
            block = jnp.dot(spread, halves, preferred_element_type=F32).astype(BF16)
            gath[z, c, :, p * LANES:(p + 1) * LANES] = block
        return 0

    def ag_copy(c, o, step, send):
        return pltpu.make_async_remote_copy(
            src_ref=gath.at[o, c], dst_ref=gath.at[o, c],
            send_sem=send.at[c, o], recv_sem=ag_recv.at[c, o],
            device_id={"mp": z + step}, device_id_type=MESH,
        )

    def ag_own(c):
        @pl.when(z < m - 1)
        def _():
            ag_copy(c, z, 1, ag_right).start()

        @pl.when(z > 0)
        def _():
            ag_copy(c, z, -1, ag_left).start()

    def ag_step(c, t):
        @pl.when(z >= t)
        def _():
            ag_copy(c, z - t, -1, ag_left).wait_recv()

            @pl.when(z < m - 1)
            def _():
                ag_copy(c, z - t, 1, ag_right).start()

        @pl.when(z + t < m)
        def _():
            ag_copy(c, z + t, 1, ag_right).wait_recv()

            @pl.when(z > 0)
            def _():
                ag_copy(c, z + t, -1, ag_left).start()

    def rs_copy(c, s, step, landing, recv):
        return pltpu.make_async_remote_copy(
            src_ref=part.at[c, s], dst_ref=landing.at[c, s],
            send_sem=rs_send.at[c, s], recv_sem=recv.at[c, s],
            device_id={"mp": z + step}, device_id_type=MESH,
        )

    def rs_stage(c, k):
        @pl.when(z == k)
        def _():
            def step(i, _):
                s = m - 1 - i
                if k > 0:
                    rs_copy(c, s, -1, from_left, rs_left).wait_recv()
                    part[c, s] = (part[c, s].astype(F32) + from_left[c, s].astype(F32)).astype(BF16)
                rs_copy(c, s, 1, from_left, rs_left).start()
                return 0

            lax.fori_loop(0, m - 1 - k, step, 0)

        @pl.when(z == m - 1 - k)
        def _():
            def step(s, _):
                if k > 0:
                    rs_copy(c, s, 1, from_right, rs_right).wait_recv()
                    part[c, s] = (part[c, s].astype(F32) + from_right[c, s].astype(F32)).astype(BF16)
                rs_copy(c, s, -1, from_right, rs_right).start()
                return 0

            lax.fori_loop(0, m - 1 - k, step, 0)

    def rs_final(c):
        total[...] = part[c, z].astype(F32)

        @pl.when(z > 0)
        def _():
            rs_copy(c, z, -1, from_left, rs_left).wait_recv()
            total[...] += from_left[c, z].astype(F32)

        @pl.when(z < m - 1)
        def _():
            rs_copy(c, z, 1, from_right, rs_right).wait_recv()
            total[...] += from_right[c, z].astype(F32)

        block = (total[...] + gath[z, c].astype(F32)).astype(BF16)
        halves = jnp.dot(gathered, block, preferred_element_type=F32)
        for p in range(PAIRS):
            even = halves[:rows, p * LANES:(p + 1) * LANES]
            odd = halves[rows:, p * LANES:(p + 1) * LANES]
            k = (c * PAIRS + p) * 2
            done[k] = jnp.where(low_half, even, pltpu.roll(odd, WIN, 1)).astype(BF16)
            done[k + 1] = jnp.where(low_half, pltpu.roll(even, WIN, 1), odd).astype(BF16)

    def project(c):
        full = gath[:, c].reshape(m * width, PAIRS * LANES).astype(F32)
        mean_square = jnp.mean(full * full, axis=0, keepdims=True)
        gain = jnp.concatenate([gain_t[...]] * PAIRS, axis=1)
        normed = (full * lax.rsqrt(mean_square + epsilon) * gain).astype(BF16)
        proj[...] = jnp.dot(qkv_t[...], normed, preferred_element_type=F32).astype(BF16)

    key_window = lax.broadcasted_iota(jnp.int32, (LANES, LANES), 0) // WIN
    query_window = lax.broadcasted_iota(jnp.int32, (LANES, LANES), 1) // WIN
    same_window = key_window == query_window

    def attend(p):
        lanes = slice(p * LANES, (p + 1) * LANES)
        for h in range(heads_here):
            base = h * 3 * HEAD_DIM
            queries = proj[base:base + HEAD_DIM, lanes]
            key_vecs = proj[base + HEAD_DIM:base + 2 * HEAD_DIM, lanes]
            value_vecs = proj[base + 2 * HEAD_DIM:base + 3 * HEAD_DIM, lanes]
            scores = lax.dot_general(
                key_vecs, queries, (((0,), (0,)), ((), ())), preferred_element_type=F32
            ) * HEAD_DIM ** (-0.5)
            scores = jnp.where(same_window, scores, -1e30)
            weights = jnp.exp(scores - jnp.max(scores, axis=0, keepdims=True))
            probs = (weights / jnp.sum(weights, axis=0, keepdims=True)).astype(BF16)
            heads[h * HEAD_DIM:(h + 1) * HEAD_DIM, lanes] = jnp.dot(
                value_vecs, probs, preferred_element_type=F32
            ).astype(BF16)

    def output(c):
        for s in range(m):
            part[c, s] = jnp.dot(
                outw_t[s * width:(s + 1) * width, :], heads[...], preferred_element_type=F32
            ).astype(BF16)

    lax.fori_loop(0, chunks, unpack, 0)
    ag_own(0)
    if chunks > 1:
        ag_own(1)
    for t in range(1, m):
        ag_step(0, t)

    between = PAIRS + 2

    def steps_at(place):
        return [t for t in range(1, m) if (t - 1) * between // (m - 1) == place]

    def turn(c, _):
        @pl.when(c + 2 < chunks)
        def _():
            ag_own(c + 2)

        for place in range(between):
            @pl.when(c < chunks)
            def _():
                if place == 0:
                    project(c)
                elif place <= PAIRS:
                    attend(place - 1)
                else:
                    output(c)

            @pl.when(c + 1 < chunks)
            def _():
                for t in steps_at(place):
                    ag_step(c + 1, t)

            @pl.when(c > 0)
            def _():
                for t in steps_at(place):
                    if t < m - 1:
                        rs_stage(c - 1, t)
                    else:
                        rs_final(c - 1)

        @pl.when(c < chunks)
        def _():
            rs_stage(c, 0)

        return 0

    lax.fori_loop(0, chunks + 1, turn, 0)

    for p in range(n):
        for j in range(cap):
            backb[p, j] = done[index_s[BACK, p * cap + j]]
        if p != own:
            exchange(backb, homeb, b_send, b_recv, p).start()
    homeb[own] = backb[own]

    def sent(c, _):
        def each(o, _):
            @pl.when(jnp.logical_and(z < m - 1, o <= z))
            def _():
                ag_copy(c, o, 1, ag_right).wait_send()

            @pl.when(jnp.logical_and(z > 0, o >= z))
            def _():
                ag_copy(c, o, -1, ag_left).wait_send()

            @pl.when(o > z)
            def _():
                rs_copy(c, o, 1, from_left, rs_left).wait_send()

            @pl.when(o < z)
            def _():
                rs_copy(c, o, -1, from_right, rs_right).wait_send()

            return 0

        return lax.fori_loop(0, m, each, 0)

    lax.fori_loop(0, chunks, sent, 0)
    for p in others:
        exchange(backb, homeb, b_send, b_recv, p).wait()

    def place_home(s, _):
        at = index_s[SLOT, s]
        safe = jnp.maximum(at, 0)
        found = homeb[safe // cap, lax.rem(safe, cap)].astype(F32)
        out_ref[s] = jnp.where(at >= 0, found, jnp.zeros_like(found)).astype(BF16)
        return 0

    lax.fori_loop(0, home_win, place_home, 0)


def body(patches, norm_gain, qkv_weight, out_weight, window_plan):
    n = lax.axis_size("dp")
    m = lax.axis_size("mp")
    home_win, row_width = patches.shape
    rows = row_width // LANES
    width = 2 * rows
    full_width = width * m
    cap = (home_win + n - 1) // n
    chunks = ENC_WIN // (2 * PAIRS)
    cols = PAIRS * LANES

    hbm = pl.BlockSpec(memory_space=pl.ANY)
    vmem = pl.BlockSpec(memory_space=pltpu.VMEM)
    dma = pltpu.SemaphoreType.DMA
    result = pl.pallas_call(
        functools.partial(kernel, n, m, cap),
        out_shape=jax.ShapeDtypeStruct((home_win, rows, LANES), BF16),
        in_specs=[vmem] * 3 + [hbm] * 2,
        out_specs=vmem,
        scratch_shapes=[
            pltpu.VMEM((8, LANES), jnp.int32),
            pltpu.SMEM((8, LANES), jnp.int32),
            pltpu.VMEM(out_weight.shape, BF16),
            pltpu.VMEM((full_width, LANES), F32),
            pltpu.VMEM((n, cap, rows, LANES), BF16),
            pltpu.VMEM((n, cap, rows, LANES), BF16),
            pltpu.VMEM((m, chunks, width, cols), BF16),
            pltpu.VMEM((qkv_weight.shape[1], full_width), BF16),
            pltpu.VMEM((full_width, out_weight.shape[0]), BF16),
            pltpu.VMEM((qkv_weight.shape[1], cols), BF16),
            pltpu.VMEM((out_weight.shape[0], cols), BF16),
            pltpu.VMEM((chunks, m, width, cols), BF16),
            pltpu.VMEM((chunks, m, width, cols), BF16),
            pltpu.VMEM((chunks, m, width, cols), BF16),
            pltpu.VMEM((width, cols), F32),
            pltpu.VMEM((ENC_WIN, rows, LANES), BF16),
            pltpu.VMEM((n, cap, rows, LANES), BF16),
            pltpu.VMEM((n, cap, rows, LANES), BF16),
            dma, dma((2,)), dma((n,)), dma((n,)), dma((n,)), dma((n,)),
            dma((chunks, m)), dma((chunks, m)), dma((chunks, m)),
            dma((chunks, m)), dma((chunks, m)), dma((chunks, m)),
        ],
        compiler_params=pltpu.CompilerParams(
            collective_id=0, has_side_effects=True, vmem_limit_bytes=56 * 1024 * 1024
        ),
    )(
        window_plan, patches.reshape(home_win, rows, LANES), norm_gain[None, :],
        qkv_weight.T, out_weight,
    )
    return result.reshape(home_win, row_width)


def solution(mesh):
    return jax.shard_map(
        body,
        mesh=mesh,
        in_specs=(P("dp", "mp"), P(), P(None, "mp"), P("mp", None), P()),
        out_specs=P("dp", "mp"),
        check_vma=False,
    )
```

```python
import functools

import jax
import jax.numpy as jnp
from jax import lax
from jax.experimental import pallas as pl
from jax.experimental.pallas import tpu as pltpu
from jax.sharding import PartitionSpec as P

HEAD_DIM = 80
WIN = 64
ENC_WIN = 16
LANES = 128
PAIRS = 1

LOG2E = 1.4426950408889634
epsilon = 1e-06
MESH = pl.DeviceIdType.MESH
F32 = jnp.float32
BF16 = jnp.bfloat16


SOURCE, CHOSEN, BACK, SLOT = range(4)


def early_positions(n, cap):
    return n - (ENC_WIN - 2 * PAIRS) // cap


def position_order(n, cap):
    far = list(range(n - 1, 1, -1))
    split = early_positions(n, cap) - 3
    return far[:split] + [1, 0] + far[split:]


def position_of(flip, n, cap):
    split = early_positions(n, cap) - 3
    at = n - 1 - flip
    at = jnp.where(at >= split, at + 2, at)
    return jnp.where(flip == 1, split, jnp.where(flip == 0, split + 1, at))


def partner(me, flip):
    other, bit = me, 1
    while bit <= flip:
        if (flip // bit) % 2:
            other = other + bit * (1 - 2 * ((me // bit) % 2))
        bit *= 2
    return other


def iota(shape, axis):
    return lax.broadcasted_iota(jnp.int32, shape, axis)


def plan_indices(n, cap, me, plan_ref, index_v):
    plan = plan_ref[...]
    index_v[...] = jnp.zeros_like(index_v)
    slots = plan.shape[1]
    mine = plan_ref[pl.ds(me, 1), :]
    same = iota((slots, slots), 0) == iota((slots, slots), 1)
    turned = jnp.sum(jnp.where(same, mine, 0), axis=1, keepdims=True)
    earlier = (turned == mine) & (iota((slots, slots), 1) < iota((slots, slots), 0))
    ordinal = jnp.sum(earlier.astype(jnp.int32), axis=1, keepdims=True)
    place = jnp.where(turned >= 0, position_of(turned ^ me, n, cap) * cap + ordinal, -1)
    grid = (slots, n * cap)
    source = jnp.sum(
        jnp.where(place == iota(grid, 1), iota(grid, 0), 0), axis=0, keepdims=True
    )
    index_v[SOURCE:SOURCE + 1, :n * cap] = jnp.clip(source, 0, slots - 1)
    index_v[SLOT:SLOT + 1, :slots] = jnp.minimum(
        jnp.sum(jnp.where(same, place, 0), axis=0, keepdims=True), n * cap - 1
    )

    counts = jnp.sum((plan == me).astype(jnp.int32), axis=1, keepdims=True)
    square = (n, n)
    counts_row = jnp.sum(
        jnp.where(iota(square, 0) == iota(square, 1), counts, 0), axis=0, keepdims=True
    )
    at_col = position_of(iota((n, 1), 0) ^ me, n, cap)
    at_row = position_of(iota((1, n), 1) ^ me, n, cap)
    offsets = jnp.sum(jnp.where(at_row < at_col, counts_row, 0), axis=1, keepdims=True)
    j = iota((n, ENC_WIN), 1) - offsets
    chosen = jnp.sum(
        jnp.where((j >= 0) & (j < counts), at_col * cap + j, 0), axis=0, keepdims=True
    )
    index_v[CHOSEN:CHOSEN + 1, :ENC_WIN] = jnp.clip(chosen, 0, n * cap - 1)
    q = iota((n, n * cap), 1)
    back = jnp.sum(
        jnp.where(q // cap == at_col, offsets + q % cap, 0), axis=0, keepdims=True
    )
    index_v[BACK:BACK + 1, :n * cap] = jnp.clip(back, 0, ENC_WIN - 1)


def kernel(
    n, m, cap,
    plan_ref, x_ref, gain_ref, qkv_ref, outw_ref,
    out_ref,
    index_v, index_s, outw, gain_t, outb, inb, gath, qkv_t, outw_t, proj, heads, part, from_left, from_right, total, done, backb, homeb,
    i_sem, w_sem, d_send, d_recv, b_send, b_recv, ag_recv, ag_right, ag_left, rs_send, rs_left, rs_right,
):
    me = lax.axis_index("dp")
    z = lax.axis_index("mp")
    home_win, rows, _ = x_ref.shape
    width = 2 * rows
    chunks = gath.shape[1]
    heads_here = qkv_ref.shape[0] // (3 * HEAD_DIM)

    order = position_order(n, cap)

    load_qkv = pltpu.make_async_copy(qkv_ref, qkv_t, w_sem.at[0])
    load_outw = pltpu.make_async_copy(outw_ref, outw, w_sem.at[1])
    load_qkv.start()
    load_outw.start()

    barrier = pltpu.get_barrier_semaphore()

    for d in range(1, n):
        pl.semaphore_signal(
            barrier, inc=1, device_id={"dp": partner(me, d)}, device_id_type=MESH
        )

    @pl.when(z > 0)
    def _():
        pl.semaphore_signal(barrier, inc=1, device_id={"mp": z - 1}, device_id_type=MESH)

    @pl.when(z < m - 1)
    def _():
        pl.semaphore_signal(barrier, inc=1, device_id={"mp": z + 1}, device_id_type=MESH)

    plan_indices(n, cap, me, plan_ref, index_v)
    load_index = pltpu.make_async_copy(index_v, index_s, i_sem)
    load_index.start()
    load_index.wait()
    for p in range(n):
        for j in range(cap):
            outb[p, j] = x_ref[index_s[SOURCE, p * cap + j]]

    ends = (z == 0).astype(jnp.int32) + (z == m - 1).astype(jnp.int32)
    pl.semaphore_wait(barrier, n + 1 - ends)

    own = order.index(0)

    def exchange(src, dst, send, recv, p):
        return pltpu.make_async_remote_copy(
            src_ref=src.at[p], dst_ref=dst.at[p], send_sem=send.at[p], recv_sem=recv.at[p],
            device_id={"dp": partner(me, order[p])}, device_id_type=MESH,
        )

    others = [p for p in range(n) if p != own]
    for p in others:
        exchange(outb, inb, d_send, d_recv, p).start()
    inb[own] = outb[own]

    load_outw.wait()
    for lower in range(0, outw.shape[1], LANES):
        outw_t[lower:lower + LANES, :] = outw[:, lower:lower + LANES].T
        gain_t[lower:lower + LANES, :] = jnp.broadcast_to(
            gain_ref[:, lower:lower + LANES], (LANES, LANES)
        ).T

    row = lax.broadcasted_iota(jnp.int32, (width, width), 0)
    col = lax.broadcasted_iota(jnp.int32, (width, width), 1)
    spread = jnp.where(
        row == jnp.where(col < rows, 2 * col, 2 * (col - rows) + 1), 1.0, 0.0
    ).astype(BF16)
    gathered = jnp.where(
        col == jnp.where(row < rows, 2 * row, 2 * (row - rows) + 1), 1.0, 0.0
    ).astype(BF16)
    low_half = lax.broadcasted_iota(jnp.int32, (rows, LANES), 1) < WIN

    for p in others:
        exchange(outb, inb, d_send, d_recv, p).wait()
    load_qkv.wait()

    def window_in(k):
        at = index_s[CHOSEN, k]
        return inb[at // cap, lax.rem(at, cap)].astype(F32)

    def unpack(c, _):
        for p in range(PAIRS):
            first = window_in((c * PAIRS + p) * 2)
            second = window_in((c * PAIRS + p) * 2 + 1)
            even = jnp.where(low_half, first, pltpu.roll(second, WIN, 1))
            odd = jnp.where(low_half, pltpu.roll(first, WIN, 1), second)
            halves = jnp.concatenate([even, odd], axis=0).astype(BF16)
            block = jnp.dot(spread, halves, preferred_element_type=F32).astype(BF16)
            gath[z, c, :, p * LANES:(p + 1) * LANES] = block
        return 0

    def ag_copy(c, o, step, send):
        return pltpu.make_async_remote_copy(
            src_ref=gath.at[o, c], dst_ref=gath.at[o, c],
            send_sem=send.at[c, o], recv_sem=ag_recv.at[c, o],
            device_id={"mp": z + step}, device_id_type=MESH,
        )

    def ag_own(c):
        @pl.when(z < m - 1)
        def _():
            ag_copy(c, z, 1, ag_right).start()

        @pl.when(z > 0)
        def _():
            ag_copy(c, z, -1, ag_left).start()

    def ag_step(c, t):
        @pl.when(z >= t)
        def _():
            ag_copy(c, z - t, -1, ag_left).wait_recv()

            @pl.when(z < m - 1)
            def _():
                ag_copy(c, z - t, 1, ag_right).start()

        @pl.when(z + t < m)
        def _():
            ag_copy(c, z + t, 1, ag_right).wait_recv()

            @pl.when(z > 0)
            def _():
                ag_copy(c, z + t, -1, ag_left).start()

    def rs_copy(c, s, step, landing, recv):
        return pltpu.make_async_remote_copy(
            src_ref=part.at[c, s], dst_ref=landing.at[c, s],
            send_sem=rs_send.at[c, s], recv_sem=recv.at[c, s],
            device_id={"mp": z + step}, device_id_type=MESH,
        )

    def rs_stage(c, k):
        @pl.when(z == k)
        def _():
            def step(i, _):
                s = m - 1 - i
                if k > 0:
                    rs_copy(c, s, -1, from_left, rs_left).wait_recv()
                    part[c, s] = (part[c, s].astype(F32) + from_left[c, s].astype(F32)).astype(BF16)
                rs_copy(c, s, 1, from_left, rs_left).start()
                return 0

            lax.fori_loop(0, m - 1 - k, step, 0)

        @pl.when(z == m - 1 - k)
        def _():
            def step(s, _):
                if k > 0:
                    rs_copy(c, s, 1, from_right, rs_right).wait_recv()
                    part[c, s] = (part[c, s].astype(F32) + from_right[c, s].astype(F32)).astype(BF16)
                rs_copy(c, s, -1, from_right, rs_right).start()
                return 0

            lax.fori_loop(0, m - 1 - k, step, 0)

    def rs_final(c):
        total[...] = part[c, z].astype(F32)

        @pl.when(z > 0)
        def _():
            rs_copy(c, z, -1, from_left, rs_left).wait_recv()
            total[...] += from_left[c, z].astype(F32)

        @pl.when(z < m - 1)
        def _():
            rs_copy(c, z, 1, from_right, rs_right).wait_recv()
            total[...] += from_right[c, z].astype(F32)

        block = (total[...] + gath[z, c].astype(F32)).astype(BF16)
        halves = jnp.dot(gathered, block, preferred_element_type=F32)
        for p in range(PAIRS):
            even = halves[:rows, p * LANES:(p + 1) * LANES]
            odd = halves[rows:, p * LANES:(p + 1) * LANES]
            k = (c * PAIRS + p) * 2
            done[k] = jnp.where(low_half, even, pltpu.roll(odd, WIN, 1)).astype(BF16)
            done[k + 1] = jnp.where(low_half, pltpu.roll(even, WIN, 1), odd).astype(BF16)

    def project(c):
        full = gath[:, c].reshape(m * width, PAIRS * LANES).astype(F32)
        mean_square = jnp.mean(full * full, axis=0, keepdims=True)
        gain = jnp.concatenate([gain_t[...]] * PAIRS, axis=1)
        normed = (full * lax.rsqrt(mean_square + epsilon) * gain).astype(BF16)
        proj[...] = jnp.dot(qkv_t[...], normed, preferred_element_type=F32).astype(BF16)

    key_window = lax.broadcasted_iota(jnp.int32, (LANES, LANES), 0) // WIN
    query_window = lax.broadcasted_iota(jnp.int32, (LANES, LANES), 1) // WIN
    same_window = key_window == query_window

    def attend(p):
        lanes = slice(p * LANES, (p + 1) * LANES)
        for h in range(heads_here):
            base = h * 3 * HEAD_DIM
            queries = proj[base:base + HEAD_DIM, lanes]
            key_vecs = proj[base + HEAD_DIM:base + 2 * HEAD_DIM, lanes]
            value_vecs = proj[base + 2 * HEAD_DIM:base + 3 * HEAD_DIM, lanes]
            scores = lax.dot_general(
                key_vecs, queries, (((0,), (0,)), ((), ())), preferred_element_type=F32
            ) * (HEAD_DIM ** (-0.5) * LOG2E)
            scores = jnp.where(same_window, scores, -1e30)
            weights = jnp.exp2(scores - jnp.max(scores, axis=0, keepdims=True))
            scale = 1.0 / jnp.sum(weights, axis=0, keepdims=True)
            probs = (weights * scale).astype(BF16)
            heads[h * HEAD_DIM:(h + 1) * HEAD_DIM, lanes] = jnp.dot(
                value_vecs, probs, preferred_element_type=F32
            ).astype(BF16)

    def output(c):
        for s in range(m):
            part[c, s] = jnp.dot(
                outw_t[s * width:(s + 1) * width, :], heads[...], preferred_element_type=F32
            ).astype(BF16)

    lax.fori_loop(0, chunks, unpack, 0)

    def within(c, act):
        @pl.when(jnp.logical_and(c >= 0, c < chunks))
        def _():
            act(c)

    def compute(c):
        project(c)
        for p in range(PAIRS):
            attend(p)
        output(c)

    def turn(i, _):
        c = i - (m - 1)
        for t in range(m - 1, 0, -1):
            within(c + m - 1 - t, lambda at, t=t: ag_step(at, t))
        within(c + m - 1, ag_own)
        within(c, compute)
        within(c, lambda at: rs_stage(at, 0))
        for k in range(1, m - 1):
            within(c - k, lambda at, k=k: rs_stage(at, k))
        within(c - (m - 1), rs_final)
        return 0

    lax.fori_loop(0, chunks + 2 * (m - 1), turn, 0)

    for p in range(n):
        for j in range(cap):
            backb[p, j] = done[index_s[BACK, p * cap + j]]
        if p != own:
            exchange(backb, homeb, b_send, b_recv, p).start()
    homeb[own] = backb[own]

    def sent(c, _):
        def each(o, _):
            @pl.when(jnp.logical_and(z < m - 1, o <= z))
            def _():
                ag_copy(c, o, 1, ag_right).wait_send()

            @pl.when(jnp.logical_and(z > 0, o >= z))
            def _():
                ag_copy(c, o, -1, ag_left).wait_send()

            @pl.when(o > z)
            def _():
                rs_copy(c, o, 1, from_left, rs_left).wait_send()

            @pl.when(o < z)
            def _():
                rs_copy(c, o, -1, from_right, rs_right).wait_send()

            return 0

        return lax.fori_loop(0, m, each, 0)

    lax.fori_loop(0, chunks, sent, 0)
    for p in others:
        exchange(backb, homeb, b_send, b_recv, p).wait()

    def place_home(s, _):
        at = index_s[SLOT, s]
        safe = jnp.maximum(at, 0)
        found = homeb[safe // cap, lax.rem(safe, cap)].astype(F32)
        out_ref[s] = jnp.where(at >= 0, found, jnp.zeros_like(found)).astype(BF16)
        return 0

    lax.fori_loop(0, home_win, place_home, 0)


def body(patches, norm_gain, qkv_weight, out_weight, window_plan):
    n = lax.axis_size("dp")
    m = lax.axis_size("mp")
    home_win, row_width = patches.shape
    rows = row_width // LANES
    width = 2 * rows
    full_width = width * m
    cap = (home_win + n - 1) // n
    chunks = ENC_WIN // (2 * PAIRS)
    cols = PAIRS * LANES

    hbm = pl.BlockSpec(memory_space=pl.ANY)
    vmem = pl.BlockSpec(memory_space=pltpu.VMEM)
    dma = pltpu.SemaphoreType.DMA
    result = pl.pallas_call(
        functools.partial(kernel, n, m, cap),
        out_shape=jax.ShapeDtypeStruct((home_win, rows, LANES), BF16),
        in_specs=[vmem] * 3 + [hbm] * 2,
        out_specs=vmem,
        scratch_shapes=[
            pltpu.VMEM((8, LANES), jnp.int32),
            pltpu.SMEM((8, LANES), jnp.int32),
            pltpu.VMEM(out_weight.shape, BF16),
            pltpu.VMEM((full_width, LANES), F32),
            pltpu.VMEM((n, cap, rows, LANES), BF16),
            pltpu.VMEM((n, cap, rows, LANES), BF16),
            pltpu.VMEM((m, chunks, width, cols), BF16),
            pltpu.VMEM((qkv_weight.shape[1], full_width), BF16),
            pltpu.VMEM((full_width, out_weight.shape[0]), BF16),
            pltpu.VMEM((qkv_weight.shape[1], cols), BF16),
            pltpu.VMEM((out_weight.shape[0], cols), BF16),
            pltpu.VMEM((chunks, m, width, cols), BF16),
            pltpu.VMEM((chunks, m, width, cols), BF16),
            pltpu.VMEM((chunks, m, width, cols), BF16),
            pltpu.VMEM((width, cols), F32),
            pltpu.VMEM((ENC_WIN, rows, LANES), BF16),
            pltpu.VMEM((n, cap, rows, LANES), BF16),
            pltpu.VMEM((n, cap, rows, LANES), BF16),
            dma, dma((2,)), dma((n,)), dma((n,)), dma((n,)), dma((n,)),
            dma((chunks, m)), dma((chunks, m)), dma((chunks, m)),
            dma((chunks, m)), dma((chunks, m)), dma((chunks, m)),
        ],
        compiler_params=pltpu.CompilerParams(
            collective_id=0, has_side_effects=True, vmem_limit_bytes=56 * 1024 * 1024
        ),
    )(
        window_plan, patches.reshape(home_win, rows, LANES), norm_gain[None, :],
        qkv_weight.T, out_weight,
    )
    return result.reshape(home_win, row_width)


def solution(mesh):
    return jax.shard_map(
        body,
        mesh=mesh,
        in_specs=(P("dp", "mp"), P(), P(None, "mp"), P("mp", None), P()),
        out_specs=P("dp", "mp"),
        check_vma=False,
    )
```

```python
import functools

import jax
import jax.numpy as jnp
from jax import lax
from jax.experimental import pallas as pl
from jax.experimental.pallas import tpu as pltpu
from jax.sharding import PartitionSpec as P

HEAD_DIM = 80
WIN = 64
ENC_WIN = 16
LANES = 128
PAIRS = 1

LOG2E = 1.4426950408889634
epsilon = 1e-06
MESH = pl.DeviceIdType.MESH
F32 = jnp.float32
BF16 = jnp.bfloat16


SOURCE, CHOSEN, BACK, SLOT = range(4)


def early_positions(n, cap):
    return n - (ENC_WIN - 2 * PAIRS) // cap


def position_order(n, cap):
    far = list(range(n - 1, 1, -1))
    split = early_positions(n, cap) - 2
    return far[:split] + [1, 0] + far[split:]


def position_of(flip, n, cap):
    split = early_positions(n, cap) - 2
    at = n - 1 - flip
    at = jnp.where(at >= split, at + 2, at)
    return jnp.where(flip == 1, split, jnp.where(flip == 0, split + 1, at))


def partner(me, flip):
    other, bit = me, 1
    while bit <= flip:
        if (flip // bit) % 2:
            other = other + bit * (1 - 2 * ((me // bit) % 2))
        bit *= 2
    return other


def iota(shape, axis):
    return lax.broadcasted_iota(jnp.int32, shape, axis)


def plan_indices(n, cap, me, plan_ref, index_v):
    plan = plan_ref[...]
    index_v[...] = jnp.zeros_like(index_v)
    slots = plan.shape[1]
    mine = plan_ref[pl.ds(me, 1), :]
    same = iota((slots, slots), 0) == iota((slots, slots), 1)
    turned = jnp.sum(jnp.where(same, mine, 0), axis=1, keepdims=True)
    earlier = (turned == mine) & (iota((slots, slots), 1) < iota((slots, slots), 0))
    ordinal = jnp.sum(earlier.astype(jnp.int32), axis=1, keepdims=True)
    place = jnp.where(turned >= 0, position_of(turned ^ me, n, cap) * cap + ordinal, -1)
    grid = (slots, n * cap)
    source = jnp.sum(
        jnp.where(place == iota(grid, 1), iota(grid, 0), 0), axis=0, keepdims=True
    )
    index_v[SOURCE:SOURCE + 1, :n * cap] = jnp.clip(source, 0, slots - 1)
    index_v[SLOT:SLOT + 1, :slots] = jnp.minimum(
        jnp.sum(jnp.where(same, place, 0), axis=0, keepdims=True), n * cap - 1
    )

    counts = jnp.sum((plan == me).astype(jnp.int32), axis=1, keepdims=True)
    square = (n, n)
    counts_row = jnp.sum(
        jnp.where(iota(square, 0) == iota(square, 1), counts, 0), axis=0, keepdims=True
    )
    at_col = position_of(iota((n, 1), 0) ^ me, n, cap)
    at_row = position_of(iota((1, n), 1) ^ me, n, cap)
    offsets = jnp.sum(jnp.where(at_row < at_col, counts_row, 0), axis=1, keepdims=True)
    j = iota((n, ENC_WIN), 1) - offsets
    chosen = jnp.sum(
        jnp.where((j >= 0) & (j < counts), at_col * cap + j, 0), axis=0, keepdims=True
    )
    index_v[CHOSEN:CHOSEN + 1, :ENC_WIN] = jnp.clip(chosen, 0, n * cap - 1)
    q = iota((n, n * cap), 1)
    back = jnp.sum(
        jnp.where(q // cap == at_col, offsets + q % cap, 0), axis=0, keepdims=True
    )
    index_v[BACK:BACK + 1, :n * cap] = jnp.clip(back, 0, ENC_WIN - 1)


def kernel(
    n, m, cap,
    plan_ref, x_ref, gain_ref, qkv_ref, outw_ref,
    out_ref,
    index_v, index_s, outw, gain_t, outb, inb, inb_late, gath, qkv_t, outw_t, proj, heads, part, from_left, from_right, total, done, backb, homeb,
    i_sem, w_sem, d_send, d_recv, b_send, b_recv, ag_recv, ag_right, ag_left, rs_send, rs_left, rs_right,
):
    me = lax.axis_index("dp")
    z = lax.axis_index("mp")
    home_win, rows, _ = x_ref.shape
    width = 2 * rows
    chunks = gath.shape[1]
    heads_here = qkv_ref.shape[0] // (3 * HEAD_DIM)

    order = position_order(n, cap)

    load_qkv = pltpu.make_async_copy(qkv_ref, qkv_t, w_sem.at[0])
    load_outw = pltpu.make_async_copy(outw_ref, outw, w_sem.at[1])
    load_qkv.start()
    load_outw.start()

    barrier = pltpu.get_barrier_semaphore()

    for d in range(1, n):
        pl.semaphore_signal(
            barrier, inc=1, device_id={"dp": partner(me, d)}, device_id_type=MESH
        )

    @pl.when(z > 0)
    def _():
        pl.semaphore_signal(barrier, inc=1, device_id={"mp": z - 1}, device_id_type=MESH)

    @pl.when(z < m - 1)
    def _():
        pl.semaphore_signal(barrier, inc=1, device_id={"mp": z + 1}, device_id_type=MESH)

    plan_indices(n, cap, me, plan_ref, index_v)
    load_index = pltpu.make_async_copy(index_v, index_s, i_sem)
    load_index.start()
    load_index.wait()
    for p in range(n):
        for j in range(cap):
            outb[p, j] = x_ref[index_s[SOURCE, p * cap + j]]

    ends = (z == 0).astype(jnp.int32) + (z == m - 1).astype(jnp.int32)
    pl.semaphore_wait(barrier, n + 1 - ends)

    own = order.index(0)

    own = order.index(0)
    early = early_positions(n, cap)

    def exchange(src, dst, send, recv, p, at):
        return pltpu.make_async_remote_copy(
            src_ref=src.at[p], dst_ref=dst.at[at], send_sem=send.at[p], recv_sem=recv.at[p],
            device_id={"dp": partner(me, order[p])}, device_id_type=MESH,
        )

    def dispatch(p):
        if p < early:
            return exchange(outb, inb, d_send, d_recv, p, p)
        return exchange(outb, inb_late, d_send, d_recv, p, p - early)

    def reply(p):
        return exchange(backb, homeb, b_send, b_recv, p, p)

    others = [p for p in range(n) if p != own]
    for p in others:
        if p < early:
            dispatch(p).start()
    inb[own] = outb[own]

    load_outw.wait()
    for lower in range(0, outw.shape[1], LANES):
        outw_t[lower:lower + LANES, :] = outw[:, lower:lower + LANES].T
        gain_t[lower:lower + LANES, :] = jnp.broadcast_to(
            gain_ref[:, lower:lower + LANES], (LANES, LANES)
        ).T

    row = lax.broadcasted_iota(jnp.int32, (width, width), 0)
    col = lax.broadcasted_iota(jnp.int32, (width, width), 1)
    spread = jnp.where(
        row == jnp.where(col < rows, 2 * col, 2 * (col - rows) + 1), 1.0, 0.0
    ).astype(BF16)
    gathered = jnp.where(
        col == jnp.where(row < rows, 2 * row, 2 * (row - rows) + 1), 1.0, 0.0
    ).astype(BF16)
    low_half = lax.broadcasted_iota(jnp.int32, (rows, LANES), 1) < WIN

    for p in others:
        if p >= early:
            dispatch(p).start()
    load_qkv.wait()
    for p in others:
        if p < early:
            dispatch(p).wait()

    def window_early(k):
        at = jnp.minimum(index_s[CHOSEN, k], early * cap - 1)
        return inb[at // cap, lax.rem(at, cap)].astype(F32)

    def window_any(k):
        at = index_s[CHOSEN, k]
        late = jnp.maximum(at - early * cap, 0)
        found = inb_late[late // cap, lax.rem(late, cap)].astype(F32)
        return jnp.where(at < early * cap, window_early(k), found)

    def unpack(c, window_in):
        for p in range(PAIRS):
            first = window_in((c * PAIRS + p) * 2)
            second = window_in((c * PAIRS + p) * 2 + 1)
            even = jnp.where(low_half, first, pltpu.roll(second, WIN, 1))
            odd = jnp.where(low_half, pltpu.roll(first, WIN, 1), second)
            halves = jnp.concatenate([even, odd], axis=0).astype(BF16)
            block = jnp.dot(spread, halves, preferred_element_type=F32).astype(BF16)
            gath[z, c, :, p * LANES:(p + 1) * LANES] = block

    def ag_copy(c, o, step, send):
        return pltpu.make_async_remote_copy(
            src_ref=gath.at[o, c], dst_ref=gath.at[o, c],
            send_sem=send.at[c, o], recv_sem=ag_recv.at[c, o],
            device_id={"mp": z + step}, device_id_type=MESH,
        )

    def ag_own(c):
        @pl.when(z < m - 1)
        def _():
            ag_copy(c, z, 1, ag_right).start()

        @pl.when(z > 0)
        def _():
            ag_copy(c, z, -1, ag_left).start()

    def ag_step(c, t):
        @pl.when(z >= t)
        def _():
            ag_copy(c, z - t, -1, ag_left).wait_recv()

            @pl.when(z < m - 1)
            def _():
                ag_copy(c, z - t, 1, ag_right).start()

        @pl.when(z + t < m)
        def _():
            ag_copy(c, z + t, 1, ag_right).wait_recv()

            @pl.when(z > 0)
            def _():
                ag_copy(c, z + t, -1, ag_left).start()

    def rs_copy(c, s, step, landing, recv):
        return pltpu.make_async_remote_copy(
            src_ref=part.at[c, s], dst_ref=landing.at[c, s],
            send_sem=rs_send.at[c, s], recv_sem=recv.at[c, s],
            device_id={"mp": z + step}, device_id_type=MESH,
        )

    def rs_stage(c, k):
        @pl.when(z == k)
        def _():
            def step(i, _):
                s = m - 1 - i
                if k > 0:
                    rs_copy(c, s, -1, from_left, rs_left).wait_recv()
                    part[c, s] = (part[c, s].astype(F32) + from_left[c, s].astype(F32)).astype(BF16)
                rs_copy(c, s, 1, from_left, rs_left).start()
                return 0

            lax.fori_loop(0, m - 1 - k, step, 0)

        @pl.when(z == m - 1 - k)
        def _():
            def step(s, _):
                if k > 0:
                    rs_copy(c, s, 1, from_right, rs_right).wait_recv()
                    part[c, s] = (part[c, s].astype(F32) + from_right[c, s].astype(F32)).astype(BF16)
                rs_copy(c, s, -1, from_right, rs_right).start()
                return 0

            lax.fori_loop(0, m - 1 - k, step, 0)

    def rs_final(c):
        total[...] = part[c, z].astype(F32)

        @pl.when(z > 0)
        def _():
            rs_copy(c, z, -1, from_left, rs_left).wait_recv()
            total[...] += from_left[c, z].astype(F32)

        @pl.when(z < m - 1)
        def _():
            rs_copy(c, z, 1, from_right, rs_right).wait_recv()
            total[...] += from_right[c, z].astype(F32)

        block = (total[...] + gath[z, c].astype(F32)).astype(BF16)
        halves = jnp.dot(gathered, block, preferred_element_type=F32)
        for p in range(PAIRS):
            even = halves[:rows, p * LANES:(p + 1) * LANES]
            odd = halves[rows:, p * LANES:(p + 1) * LANES]
            k = (c * PAIRS + p) * 2
            done[k] = jnp.where(low_half, even, pltpu.roll(odd, WIN, 1)).astype(BF16)
            done[k + 1] = jnp.where(low_half, pltpu.roll(even, WIN, 1), odd).astype(BF16)

    def project(c):
        full = gath[:, c].reshape(m * width, PAIRS * LANES).astype(F32)
        mean_square = jnp.mean(full * full, axis=0, keepdims=True)
        gain = jnp.concatenate([gain_t[...]] * PAIRS, axis=1)
        normed = (full * lax.rsqrt(mean_square + epsilon) * gain).astype(BF16)
        proj[...] = jnp.dot(qkv_t[...], normed, preferred_element_type=F32).astype(BF16)

    key_window = lax.broadcasted_iota(jnp.int32, (LANES, LANES), 0) // WIN
    query_window = lax.broadcasted_iota(jnp.int32, (LANES, LANES), 1) // WIN
    same_window = key_window == query_window

    def attend(p):
        lanes = slice(p * LANES, (p + 1) * LANES)
        for h in range(heads_here):
            base = h * 3 * HEAD_DIM
            queries = proj[base:base + HEAD_DIM, lanes]
            key_vecs = proj[base + HEAD_DIM:base + 2 * HEAD_DIM, lanes]
            value_vecs = proj[base + 2 * HEAD_DIM:base + 3 * HEAD_DIM, lanes]
            scores = lax.dot_general(
                key_vecs, queries, (((0,), (0,)), ((), ())), preferred_element_type=F32
            ) * (HEAD_DIM ** (-0.5) * LOG2E)
            scores = jnp.where(same_window, scores, -1e30)
            weights = jnp.exp2(scores - jnp.max(scores, axis=0, keepdims=True))
            scale = 1.0 / jnp.sum(weights, axis=0, keepdims=True)
            probs = (weights * scale).astype(BF16)
            heads[h * HEAD_DIM:(h + 1) * HEAD_DIM, lanes] = jnp.dot(
                value_vecs, probs, preferred_element_type=F32
            ).astype(BF16)

    def output(c):
        for s in range(m):
            part[c, s] = jnp.dot(
                outw_t[s * width:(s + 1) * width, :], heads[...], preferred_element_type=F32
            ).astype(BF16)

    chunk_win = 2 * PAIRS
    early_chunks = sum(
        n - (ENC_WIN - (c + 1) * chunk_win) // cap <= early for c in range(chunks)
    )

    def own_chunk(c):
        @pl.when(c < early_chunks)
        def _():
            unpack(c, window_early)

        if early_chunks < chunks:
            @pl.when(c == early_chunks)
            def _():
                for p in others:
                    if p >= early:
                        dispatch(p).wait()

            @pl.when(c >= early_chunks)
            def _():
                unpack(c, window_any)

        ag_own(c)

    def ready(p):
        return (min(ENC_WIN, cap * (p + 1)) - 1) // chunk_win

    def answer(p):
        for j in range(cap):
            backb[p, j] = done[index_s[BACK, p * cap + j]]
        if p != own:
            reply(p).start()

    def finish(c):
        rs_final(c)
        for p in range(n):
            if ready(p) < chunks - 1:
                pl.when(c == ready(p))(functools.partial(answer, p))


    def within(c, act):
        @pl.when(jnp.logical_and(c >= 0, c < chunks))
        def _():
            act(c)

    def compute(c):
        project(c)
        for p in range(PAIRS):
            attend(p)
        output(c)

    def turn(i, _):
        c = i - (m - 1)
        for t in range(m - 1, 0, -1):
            within(c + m - 1 - t, lambda at, t=t: ag_step(at, t))
        within(c + m - 1, own_chunk)
        within(c, compute)
        within(c, lambda at: rs_stage(at, 0))
        for k in range(1, m - 1):
            within(c - k, lambda at, k=k: rs_stage(at, k))
        within(c - (m - 1), finish)
        return 0

    lax.fori_loop(0, chunks + 2 * (m - 1), turn, 0)

    for p in range(n):
        if ready(p) == chunks - 1:
            answer(p)
    homeb[own] = backb[own]

    def sent(c, _):
        def each(o, _):
            @pl.when(jnp.logical_and(z < m - 1, o <= z))
            def _():
                ag_copy(c, o, 1, ag_right).wait_send()

            @pl.when(jnp.logical_and(z > 0, o >= z))
            def _():
                ag_copy(c, o, -1, ag_left).wait_send()

            @pl.when(o > z)
            def _():
                rs_copy(c, o, 1, from_left, rs_left).wait_send()

            @pl.when(o < z)
            def _():
                rs_copy(c, o, -1, from_right, rs_right).wait_send()

            return 0

        return lax.fori_loop(0, m, each, 0)

    lax.fori_loop(0, chunks, sent, 0)
    for p in others:
        reply(p).wait()

    def place_home(s, _):
        at = index_s[SLOT, s]
        safe = jnp.maximum(at, 0)
        found = homeb[safe // cap, lax.rem(safe, cap)].astype(F32)
        out_ref[s] = jnp.where(at >= 0, found, jnp.zeros_like(found)).astype(BF16)
        return 0

    lax.fori_loop(0, home_win, place_home, 0)


def body(patches, norm_gain, qkv_weight, out_weight, window_plan):
    n = lax.axis_size("dp")
    m = lax.axis_size("mp")
    home_win, row_width = patches.shape
    rows = row_width // LANES
    width = 2 * rows
    full_width = width * m
    cap = (home_win + n - 1) // n
    chunks = ENC_WIN // (2 * PAIRS)
    cols = PAIRS * LANES
    early = early_positions(n, cap)

    hbm = pl.BlockSpec(memory_space=pl.ANY)
    vmem = pl.BlockSpec(memory_space=pltpu.VMEM)
    dma = pltpu.SemaphoreType.DMA
    result = pl.pallas_call(
        functools.partial(kernel, n, m, cap),
        out_shape=jax.ShapeDtypeStruct((home_win, rows, LANES), BF16),
        in_specs=[vmem] * 3 + [hbm] * 2,
        out_specs=vmem,
        scratch_shapes=[
            pltpu.VMEM((8, LANES), jnp.int32),
            pltpu.SMEM((8, LANES), jnp.int32),
            pltpu.VMEM(out_weight.shape, BF16),
            pltpu.VMEM((full_width, LANES), F32),
            pltpu.VMEM((n, cap, rows, LANES), BF16),
            pltpu.VMEM((early, cap, rows, LANES), BF16),
            pltpu.VMEM((n - early, cap, rows, LANES), BF16),
            pltpu.VMEM((m, chunks, width, cols), BF16),
            pltpu.VMEM((qkv_weight.shape[1], full_width), BF16),
            pltpu.VMEM((full_width, out_weight.shape[0]), BF16),
            pltpu.VMEM((qkv_weight.shape[1], cols), BF16),
            pltpu.VMEM((out_weight.shape[0], cols), BF16),
            pltpu.VMEM((chunks, m, width, cols), BF16),
            pltpu.VMEM((chunks, m, width, cols), BF16),
            pltpu.VMEM((chunks, m, width, cols), BF16),
            pltpu.VMEM((width, cols), F32),
            pltpu.VMEM((ENC_WIN, rows, LANES), BF16),
            pltpu.VMEM((n, cap, rows, LANES), BF16),
            pltpu.VMEM((n, cap, rows, LANES), BF16),
            dma, dma((2,)), dma((n,)), dma((n,)), dma((n,)), dma((n,)),
            dma((chunks, m)), dma((chunks, m)), dma((chunks, m)),
            dma((chunks, m)), dma((chunks, m)), dma((chunks, m)),
        ],
        compiler_params=pltpu.CompilerParams(
            collective_id=0, has_side_effects=True, vmem_limit_bytes=56 * 1024 * 1024
        ),
    )(
        window_plan, patches.reshape(home_win, rows, LANES), norm_gain[None, :],
        qkv_weight.T, out_weight,
    )
    return result.reshape(home_win, row_width)


def solution(mesh):
    return jax.shard_map(
        body,
        mesh=mesh,
        in_specs=(P("dp", "mp"), P(), P(None, "mp"), P("mp", None), P()),
        out_specs=P("dp", "mp"),
        check_vma=False,
    )
```

```python
import functools

import jax
import jax.numpy as jnp
from jax import lax
from jax.experimental import pallas as pl
from jax.experimental.pallas import tpu as pltpu
from jax.sharding import PartitionSpec as P

HEAD_DIM = 80
WIN = 64
ENC_WIN = 16
LANES = 128
PAIRS = 1

LOG2E = 1.4426950408889634
epsilon = 1e-06
MESH = pl.DeviceIdType.MESH
F32 = jnp.float32
BF16 = jnp.bfloat16


SOURCE, CHOSEN, BACK, SLOT = range(4)


def early_positions(n, cap):
    return n - (ENC_WIN - 2 * PAIRS) // cap


def position_order(n, cap):
    far = list(range(n - 2, 1, -2)) + list(range(n - 1, 2, -2))
    split = early_positions(n, cap) - 2
    return far[:split] + [1, 0] + far[split:]


def position_of(flip, n, cap):
    split = early_positions(n, cap) - 2
    at = jnp.where(flip % 2 == 0, (n - 2 - flip) // 2, n // 2 - 1 + (n - 1 - flip) // 2)
    at = jnp.where(at >= split, at + 2, at)
    return jnp.where(flip == 1, split, jnp.where(flip == 0, split + 1, at))


def partner(me, flip):
    other, bit = me, 1
    while bit <= flip:
        if (flip // bit) % 2:
            other = other + bit * (1 - 2 * ((me // bit) % 2))
        bit *= 2
    return other


def iota(shape, axis):
    return lax.broadcasted_iota(jnp.int32, shape, axis)


def plan_indices(n, cap, me, plan_ref, index_v):
    plan = plan_ref[...]
    index_v[...] = jnp.zeros_like(index_v)
    slots = plan.shape[1]
    mine = plan_ref[pl.ds(me, 1), :]
    same = iota((slots, slots), 0) == iota((slots, slots), 1)
    turned = jnp.sum(jnp.where(same, mine, 0), axis=1, keepdims=True)
    earlier = (turned == mine) & (iota((slots, slots), 1) < iota((slots, slots), 0))
    ordinal = jnp.sum(earlier.astype(jnp.int32), axis=1, keepdims=True)
    place = jnp.where(turned >= 0, position_of(turned ^ me, n, cap) * cap + ordinal, n * cap)
    grid = (slots, n * cap)
    source = jnp.sum(
        jnp.where(place == iota(grid, 1), iota(grid, 0), 0), axis=0, keepdims=True
    )
    index_v[SOURCE:SOURCE + 1, :n * cap] = jnp.clip(source, 0, slots - 1)
    index_v[SLOT:SLOT + 1, :slots] = jnp.minimum(
        jnp.sum(jnp.where(same, place, 0), axis=0, keepdims=True), n * cap
    )

    counts = jnp.sum((plan == me).astype(jnp.int32), axis=1, keepdims=True)
    square = (n, n)
    counts_row = jnp.sum(
        jnp.where(iota(square, 0) == iota(square, 1), counts, 0), axis=0, keepdims=True
    )
    at_col = position_of(iota((n, 1), 0) ^ me, n, cap)
    at_row = position_of(iota((1, n), 1) ^ me, n, cap)
    offsets = jnp.sum(jnp.where(at_row < at_col, counts_row, 0), axis=1, keepdims=True)
    j = iota((n, ENC_WIN), 1) - offsets
    chosen = jnp.sum(
        jnp.where((j >= 0) & (j < counts), at_col * cap + j, 0), axis=0, keepdims=True
    )
    index_v[CHOSEN:CHOSEN + 1, :ENC_WIN] = jnp.clip(chosen, 0, n * cap - 1)
    q = iota((n, n * cap), 1)
    back = jnp.sum(
        jnp.where(q // cap == at_col, offsets + q % cap, 0), axis=0, keepdims=True
    )
    index_v[BACK:BACK + 1, :n * cap] = jnp.clip(back, 0, ENC_WIN - 1)


def kernel(
    n, m, cap,
    plan_ref, x_ref, gain_ref, qkv_ref, outw_ref,
    out_ref,
    index_v, index_s, outw, gain_t, outb, inb, inb_late, gath, qkv_t, outw_t, proj, heads, part, from_left, from_right, total, done, backb, homeb,
    i_sem, w_sem, d_send, d_recv, b_send, b_recv, ag_recv, ag_right, ag_left, rs_send, rs_left, rs_right,
):
    me = lax.axis_index("dp")
    z = lax.axis_index("mp")
    home_win, rows, _ = x_ref.shape
    width = 2 * rows
    chunks = gath.shape[1]
    heads_here = qkv_ref.shape[0] // (3 * HEAD_DIM)

    order = position_order(n, cap)

    load_qkv = pltpu.make_async_copy(qkv_ref, qkv_t, w_sem.at[0])
    load_outw = pltpu.make_async_copy(outw_ref, outw, w_sem.at[1])
    load_qkv.start()
    load_outw.start()

    barrier = pltpu.get_barrier_semaphore()

    for d in range(1, n):
        pl.semaphore_signal(
            barrier, inc=1, device_id={"dp": partner(me, d)}, device_id_type=MESH
        )

    @pl.when(z > 0)
    def _():
        pl.semaphore_signal(barrier, inc=1, device_id={"mp": z - 1}, device_id_type=MESH)

    @pl.when(z < m - 1)
    def _():
        pl.semaphore_signal(barrier, inc=1, device_id={"mp": z + 1}, device_id_type=MESH)

    plan_indices(n, cap, me, plan_ref, index_v)
    load_index = pltpu.make_async_copy(index_v, index_s, i_sem)
    load_index.start()
    load_index.wait()
    for p in range(n):
        for j in range(cap):
            outb[p, j] = x_ref[index_s[SOURCE, p * cap + j]]

    ends = (z == 0).astype(jnp.int32) + (z == m - 1).astype(jnp.int32)
    pl.semaphore_wait(barrier, n + 1 - ends)

    own = order.index(0)

    own = order.index(0)
    early = early_positions(n, cap)

    def exchange(src, dst, send, recv, p, at):
        return pltpu.make_async_remote_copy(
            src_ref=src.at[p], dst_ref=dst.at[at], send_sem=send.at[p], recv_sem=recv.at[p],
            device_id={"dp": partner(me, order[p])}, device_id_type=MESH,
        )

    def dispatch(p):
        if p < early:
            return exchange(outb, inb, d_send, d_recv, p, p)
        return exchange(outb, inb_late, d_send, d_recv, p, p - early)

    def reply(p):
        return exchange(backb, homeb, b_send, b_recv, p, p)

    others = [p for p in range(n) if p != own]
    for p in others:
        if p < early:
            dispatch(p).start()
    inb[own] = outb[own]

    load_outw.wait()
    for lower in range(0, outw.shape[1], LANES):
        outw_t[lower:lower + LANES, :] = outw[:, lower:lower + LANES].T
        gain_t[lower:lower + LANES, :] = jnp.broadcast_to(
            gain_ref[lower // LANES:lower // LANES + 1, :], (LANES, LANES)
        ).T

    row = lax.broadcasted_iota(jnp.int32, (width, width), 0)
    col = lax.broadcasted_iota(jnp.int32, (width, width), 1)
    spread = jnp.where(
        row == jnp.where(col < rows, 2 * col, 2 * (col - rows) + 1), 1.0, 0.0
    ).astype(BF16)
    gathered = jnp.where(
        col == jnp.where(row < rows, 2 * row, 2 * (row - rows) + 1), 1.0, 0.0
    ).astype(BF16)
    low_half = lax.broadcasted_iota(jnp.int32, (rows, LANES), 1) < WIN

    for p in others:
        if p >= early:
            dispatch(p).start()
    load_qkv.wait()
    for p in others:
        if p < early:
            dispatch(p).wait()

    def window_early(k):
        at = jnp.minimum(index_s[CHOSEN, k], early * cap - 1)
        return inb[at // cap, lax.rem(at, cap)].astype(F32)

    def window_any(k):
        at = index_s[CHOSEN, k]
        late = jnp.maximum(at - early * cap, 0)
        found = inb_late[late // cap, lax.rem(late, cap)].astype(F32)
        return jnp.where(at < early * cap, window_early(k), found)

    def unpack(c, window_in):
        for p in range(PAIRS):
            first = window_in((c * PAIRS + p) * 2)
            second = window_in((c * PAIRS + p) * 2 + 1)
            even = jnp.where(low_half, first, pltpu.roll(second, WIN, 1))
            odd = jnp.where(low_half, pltpu.roll(first, WIN, 1), second)
            halves = jnp.concatenate([even, odd], axis=0).astype(BF16)
            block = jnp.dot(spread, halves, preferred_element_type=F32).astype(BF16)
            gath[z, c, :, p * LANES:(p + 1) * LANES] = block

    def ag_copy(c, o, step, send):
        return pltpu.make_async_remote_copy(
            src_ref=gath.at[o, c], dst_ref=gath.at[o, c],
            send_sem=send.at[c, o], recv_sem=ag_recv.at[c, o],
            device_id={"mp": z + step}, device_id_type=MESH,
        )

    def ag_own(c):
        @pl.when(z < m - 1)
        def _():
            ag_copy(c, z, 1, ag_right).start()

        @pl.when(z > 0)
        def _():
            ag_copy(c, z, -1, ag_left).start()

    def ag_step(c, t):
        @pl.when(z >= t)
        def _():
            ag_copy(c, z - t, -1, ag_left).wait_recv()

            @pl.when(z < m - 1)
            def _():
                ag_copy(c, z - t, 1, ag_right).start()

        @pl.when(z + t < m)
        def _():
            ag_copy(c, z + t, 1, ag_right).wait_recv()

            @pl.when(z > 0)
            def _():
                ag_copy(c, z + t, -1, ag_left).start()

    def rs_copy(c, s, step, landing, recv):
        return pltpu.make_async_remote_copy(
            src_ref=part.at[c, s], dst_ref=landing.at[c, s],
            send_sem=rs_send.at[c, s], recv_sem=recv.at[c, s],
            device_id={"mp": z + step}, device_id_type=MESH,
        )

    def rs_stage(c, k):
        @pl.when(z == k)
        def _():
            def step(i, _):
                s = m - 1 - i
                if k > 0:
                    rs_copy(c, s, -1, from_left, rs_left).wait_recv()
                    part[c, s] = (part[c, s].astype(F32) + from_left[c, s].astype(F32)).astype(BF16)
                rs_copy(c, s, 1, from_left, rs_left).start()
                return 0

            lax.fori_loop(0, m - 1 - k, step, 0)

        @pl.when(z == m - 1 - k)
        def _():
            def step(s, _):
                if k > 0:
                    rs_copy(c, s, 1, from_right, rs_right).wait_recv()
                    part[c, s] = (part[c, s].astype(F32) + from_right[c, s].astype(F32)).astype(BF16)
                rs_copy(c, s, -1, from_right, rs_right).start()
                return 0

            lax.fori_loop(0, m - 1 - k, step, 0)

    def rs_final(c):
        total[...] = part[c, z].astype(F32)

        @pl.when(z > 0)
        def _():
            rs_copy(c, z, -1, from_left, rs_left).wait_recv()
            total[...] += from_left[c, z].astype(F32)

        @pl.when(z < m - 1)
        def _():
            rs_copy(c, z, 1, from_right, rs_right).wait_recv()
            total[...] += from_right[c, z].astype(F32)

        block = (total[...] + gath[z, c].astype(F32)).astype(BF16)
        halves = jnp.dot(gathered, block, preferred_element_type=F32)
        for p in range(PAIRS):
            even = halves[:rows, p * LANES:(p + 1) * LANES]
            odd = halves[rows:, p * LANES:(p + 1) * LANES]
            k = (c * PAIRS + p) * 2
            done[k] = jnp.where(low_half, even, pltpu.roll(odd, WIN, 1)).astype(BF16)
            done[k + 1] = jnp.where(low_half, pltpu.roll(even, WIN, 1), odd).astype(BF16)

    def project(c):
        full = gath[:, c].reshape(m * width, PAIRS * LANES).astype(F32)
        mean_square = jnp.mean(full * full, axis=0, keepdims=True)
        gain = jnp.concatenate([gain_t[...]] * PAIRS, axis=1)
        normed = (full * lax.rsqrt(mean_square + epsilon) * gain).astype(BF16)
        proj[...] = jnp.dot(qkv_t[...], normed, preferred_element_type=F32).astype(BF16)

    first_window = iota((WIN, LANES), 1) < WIN

    def attend(p):
        lanes = slice(p * LANES, (p + 1) * LANES)
        for h in range(heads_here):
            base = h * 3 * HEAD_DIM
            queries = proj[base:base + HEAD_DIM, lanes]
            key_vecs = proj[base + HEAD_DIM:base + 2 * HEAD_DIM, lanes]
            value_vecs = proj[base + 2 * HEAD_DIM:base + 3 * HEAD_DIM, lanes]
            scores = lax.dot_general(
                key_vecs, queries, (((0,), (0,)), ((), ())), preferred_element_type=F32
            ) * (HEAD_DIM ** (-0.5) * LOG2E)
            scores = jnp.where(first_window, scores[:WIN], scores[WIN:])
            weights = jnp.exp2(scores - jnp.max(scores, axis=0, keepdims=True))
            scale = 1.0 / jnp.sum(weights, axis=0, keepdims=True)
            probs = weights * scale
            probs = jnp.concatenate(
                [jnp.where(first_window, probs, 0.0), jnp.where(first_window, 0.0, probs)], axis=0
            ).astype(BF16)
            heads[h * HEAD_DIM:(h + 1) * HEAD_DIM, lanes] = jnp.dot(
                value_vecs, probs, preferred_element_type=F32
            ).astype(BF16)

    def output(c):
        for s in range(m):
            part[c, s] = jnp.dot(
                outw_t[s * width:(s + 1) * width, :], heads[...], preferred_element_type=F32
            ).astype(BF16)

    chunk_win = 2 * PAIRS
    early_chunks = sum(
        n - (ENC_WIN - (c + 1) * chunk_win) // cap <= early for c in range(chunks)
    )

    def own_chunk(c):
        @pl.when(c < early_chunks)
        def _():
            unpack(c, window_early)

        if early_chunks < chunks:
            @pl.when(c == early_chunks)
            def _():
                for p in others:
                    if p >= early:
                        dispatch(p).wait()

            @pl.when(c >= early_chunks)
            def _():
                unpack(c, window_any)

        ag_own(c)

    def ready(p):
        return (min(ENC_WIN, cap * (p + 1)) - 1) // chunk_win

    def answer(p):
        for j in range(cap):
            backb[p, j] = done[index_s[BACK, p * cap + j]]
        if p != own:
            reply(p).start()

    def finish(c):
        rs_final(c)
        for p in range(n):
            if ready(p) < chunks - 1:
                pl.when(c == ready(p))(functools.partial(answer, p))


    def within(c, act):
        @pl.when(jnp.logical_and(c >= 0, c < chunks))
        def _():
            act(c)

    def compute(c):
        project(c)
        for p in range(PAIRS):
            attend(p)
        output(c)

    def turn(i, _):
        c = i - (m - 1)
        for t in range(m - 1, 0, -1):
            within(c + m - 1 - t, lambda at, t=t: ag_step(at, t))
        within(c + m - 1, own_chunk)
        within(c, compute)
        within(c, lambda at: rs_stage(at, 0))
        for k in range(1, m - 1):
            within(c - k, lambda at, k=k: rs_stage(at, k))
        within(c - (m - 1), finish)
        return 0

    lax.fori_loop(0, chunks + 2 * (m - 1), turn, 0)

    for p in range(n):
        if ready(p) == chunks - 1:
            answer(p)
    homeb[own] = backb[own]
    homeb[n] = jnp.zeros_like(homeb[n])

    def sent(c, _):
        def each(o, _):
            @pl.when(jnp.logical_and(z < m - 1, o <= z))
            def _():
                ag_copy(c, o, 1, ag_right).wait_send()

            @pl.when(jnp.logical_and(z > 0, o >= z))
            def _():
                ag_copy(c, o, -1, ag_left).wait_send()

            @pl.when(o > z)
            def _():
                rs_copy(c, o, 1, from_left, rs_left).wait_send()

            @pl.when(o < z)
            def _():
                rs_copy(c, o, -1, from_right, rs_right).wait_send()

            return 0

        return lax.fori_loop(0, m, each, 0)

    lax.fori_loop(0, chunks, sent, 0)
    for p in others:
        reply(p).wait()

    def place_home(s, _):
        at = index_s[SLOT, s]
        out_ref[s] = homeb[at // cap, lax.rem(at, cap)]
        return 0

    lax.fori_loop(0, home_win, place_home, 0)


def body(patches, norm_gain, qkv_weight, out_weight, window_plan):
    n = lax.axis_size("dp")
    m = lax.axis_size("mp")
    home_win, row_width = patches.shape
    rows = row_width // LANES
    width = 2 * rows
    full_width = width * m
    cap = (home_win + n - 1) // n
    chunks = ENC_WIN // (2 * PAIRS)
    cols = PAIRS * LANES
    early = early_positions(n, cap)

    hbm = pl.BlockSpec(memory_space=pl.ANY)
    vmem = pl.BlockSpec(memory_space=pltpu.VMEM)
    dma = pltpu.SemaphoreType.DMA
    result = pl.pallas_call(
        functools.partial(kernel, n, m, cap),
        out_shape=jax.ShapeDtypeStruct((home_win, rows, LANES), BF16),
        in_specs=[vmem] * 3 + [hbm] * 2,
        out_specs=vmem,
        scratch_shapes=[
            pltpu.VMEM((8, LANES), jnp.int32),
            pltpu.SMEM((8, LANES), jnp.int32),
            pltpu.VMEM(out_weight.shape, BF16),
            pltpu.VMEM((full_width, LANES), F32),
            pltpu.VMEM((n, cap, rows, LANES), BF16),
            pltpu.VMEM((early, cap, rows, LANES), BF16),
            pltpu.VMEM((n - early, cap, rows, LANES), BF16),
            pltpu.VMEM((m, chunks, width, cols), BF16),
            pltpu.VMEM((qkv_weight.shape[1], full_width), BF16),
            pltpu.VMEM((full_width, out_weight.shape[0]), BF16),
            pltpu.VMEM((qkv_weight.shape[1], cols), BF16),
            pltpu.VMEM((out_weight.shape[0], cols), BF16),
            pltpu.VMEM((chunks, m, width, cols), BF16),
            pltpu.VMEM((chunks, m, width, cols), BF16),
            pltpu.VMEM((chunks, m, width, cols), BF16),
            pltpu.VMEM((width, cols), F32),
            pltpu.VMEM((ENC_WIN, rows, LANES), BF16),
            pltpu.VMEM((n, cap, rows, LANES), BF16),
            pltpu.VMEM((n + 1, cap, rows, LANES), BF16),
            dma, dma((2,)), dma((n,)), dma((n,)), dma((n,)), dma((n,)),
            dma((chunks, m)), dma((chunks, m)), dma((chunks, m)),
            dma((chunks, m)), dma((chunks, m)), dma((chunks, m)),
        ],
        compiler_params=pltpu.CompilerParams(
            collective_id=0, has_side_effects=True, vmem_limit_bytes=56 * 1024 * 1024
        ),
    )(
        window_plan, patches.reshape(home_win, rows, LANES), norm_gain.reshape(-1, LANES),
        qkv_weight.T, out_weight,
    )
    return result.reshape(home_win, row_width)


def solution(mesh):
    return jax.shard_map(
        body,
        mesh=mesh,
        in_specs=(P("dp", "mp"), P(), P(None, "mp"), P("mp", None), P()),
        out_specs=P("dp", "mp"),
        check_vma=False,
    )
```

```python
import functools

import jax
import jax.numpy as jnp
from jax import lax
from jax.experimental import pallas as pl
from jax.experimental.pallas import tpu as pltpu
from jax.sharding import PartitionSpec as P

HEAD_DIM = 80
WIN = 64
ENC_WIN = 16
LANES = 128
PAIRS = 1

LOG2E = 1.4426950408889634
epsilon = 1e-06
MESH = pl.DeviceIdType.MESH
F32 = jnp.float32
BF16 = jnp.bfloat16


SOURCE, CHOSEN, BACK, SLOT = range(4)


def early_positions(n, cap):
    return n - (ENC_WIN - 2 * PAIRS) // cap


def arrival_stages(n, cap):
    early, reach = early_positions(n, cap), min(cap, 2 * PAIRS)
    stages = [(0, early, 0, reach), (0, early, reach, cap)]
    stages += [(early, early + 1, 0, cap), (early + 1, n, 0, cap)]
    return [part for part in stages if part[0] < part[1] and part[2] < part[3]]


def early_stages(n, cap):
    return sum(part[0] == 0 for part in arrival_stages(n, cap))


def stages_needed(n, cap, c):
    last = (c + 1) * 2 * PAIRS - 1
    positions = n - (ENC_WIN - 1 - last) // cap
    return max(
        at + 1
        for at, (low, _, first, _) in enumerate(arrival_stages(n, cap))
        if low < positions and first <= last
    )


def position_order(n, cap):
    far = list(range(n - 2, 1, -2)) + list(range(n - 1, 2, -2))
    split = early_positions(n, cap) - 2
    return far[:split] + [1, 0] + far[split:]


def position_of(flip, n, cap):
    split = early_positions(n, cap) - 2
    at = jnp.where(flip % 2 == 0, (n - 2 - flip) // 2, n // 2 - 1 + (n - 1 - flip) // 2)
    at = jnp.where(at >= split, at + 2, at)
    return jnp.where(flip == 1, split, jnp.where(flip == 0, split + 1, at))


def partner(me, flip):
    other, bit = me, 1
    while bit <= flip:
        if (flip // bit) % 2:
            other = other + bit * (1 - 2 * ((me // bit) % 2))
        bit *= 2
    return other


def iota(shape, axis):
    return lax.broadcasted_iota(jnp.int32, shape, axis)


def plan_indices(n, cap, me, plan_ref, index_v):
    plan = plan_ref[...]
    index_v[...] = jnp.zeros_like(index_v)
    slots = plan.shape[1]
    mine = plan_ref[pl.ds(me, 1), :]
    same = iota((slots, slots), 0) == iota((slots, slots), 1)
    turned = jnp.sum(jnp.where(same, mine, 0), axis=1, keepdims=True)
    earlier = (turned == mine) & (iota((slots, slots), 1) < iota((slots, slots), 0))
    ordinal = jnp.sum(earlier.astype(jnp.int32), axis=1, keepdims=True)
    place = jnp.where(turned >= 0, position_of(turned ^ me, n, cap) * cap + ordinal, n * cap)
    grid = (slots, n * cap)
    source = jnp.sum(
        jnp.where(place == iota(grid, 1), iota(grid, 0), 0), axis=0, keepdims=True
    )
    index_v[SOURCE:SOURCE + 1, :n * cap] = jnp.clip(source, 0, slots - 1)
    index_v[SLOT:SLOT + 1, :slots] = jnp.minimum(
        jnp.sum(jnp.where(same, place, 0), axis=0, keepdims=True), n * cap
    )

    counts = jnp.sum((plan == me).astype(jnp.int32), axis=1, keepdims=True)
    square = (n, n)
    counts_row = jnp.sum(
        jnp.where(iota(square, 0) == iota(square, 1), counts, 0), axis=0, keepdims=True
    )
    at_col = position_of(iota((n, 1), 0) ^ me, n, cap)
    at_row = position_of(iota((1, n), 1) ^ me, n, cap)
    offsets = jnp.sum(jnp.where(at_row < at_col, counts_row, 0), axis=1, keepdims=True)
    j = iota((n, ENC_WIN), 1) - offsets
    chosen = jnp.sum(
        jnp.where((j >= 0) & (j < counts), at_col * cap + j, 0), axis=0, keepdims=True
    )
    index_v[CHOSEN:CHOSEN + 1, :ENC_WIN] = jnp.clip(chosen, 0, n * cap - 1)
    q = iota((n, n * cap), 1)
    back = jnp.sum(
        jnp.where(q // cap == at_col, offsets + q % cap, 0), axis=0, keepdims=True
    )
    index_v[BACK:BACK + 1, :n * cap] = jnp.clip(back, 0, ENC_WIN - 1)


def kernel(
    n, m, cap,
    plan_ref, x_ref, gain_ref, qkv_ref, outw_ref,
    out_ref,
    index_v, index_s, outw, gain_t, outb, inbs, gath, qkv_t, outw_t, proj, heads, part, from_left, from_right, total, done, backb, homeb,
    i_sem, w_sem, d_send, d_recv, b_send, b_recv, ag_recv, ag_right, ag_left, rs_send, rs_left, rs_right,
):
    me = lax.axis_index("dp")
    z = lax.axis_index("mp")
    home_win, rows, _ = x_ref.shape
    width = 2 * rows
    chunks = gath.shape[1]
    heads_here = qkv_ref.shape[0] // (3 * HEAD_DIM)

    order = position_order(n, cap)

    load_qkv = pltpu.make_async_copy(qkv_ref, qkv_t, w_sem.at[0])
    load_outw = pltpu.make_async_copy(outw_ref, outw, w_sem.at[1])
    load_qkv.start()
    load_outw.start()

    barrier = pltpu.get_barrier_semaphore()

    for d in range(1, n):
        pl.semaphore_signal(
            barrier, inc=1, device_id={"dp": partner(me, d)}, device_id_type=MESH
        )

    @pl.when(z > 0)
    def _():
        pl.semaphore_signal(barrier, inc=1, device_id={"mp": z - 1}, device_id_type=MESH)

    @pl.when(z < m - 1)
    def _():
        pl.semaphore_signal(barrier, inc=1, device_id={"mp": z + 1}, device_id_type=MESH)

    plan_indices(n, cap, me, plan_ref, index_v)
    load_index = pltpu.make_async_copy(index_v, index_s, i_sem)
    load_index.start()
    load_index.wait()
    for p in range(n):
        for j in range(cap):
            outb[p, j] = x_ref[index_s[SOURCE, p * cap + j]]

    ends = (z == 0).astype(jnp.int32) + (z == m - 1).astype(jnp.int32)
    pl.semaphore_wait(barrier, n + 1 - ends)

    own = order.index(0)

    own = order.index(0)
    stages = arrival_stages(n, cap)
    begun = early_stages(n, cap)

    def exchange(src, dst, send, recv, p, at):
        return pltpu.make_async_remote_copy(
            src_ref=src.at[p], dst_ref=dst.at[at], send_sem=send.at[p], recv_sem=recv.at[p],
            device_id={"dp": partner(me, order[p])}, device_id_type=MESH,
        )

    def dispatch(stage, p):
        low, _, first, end = stages[stage]
        return pltpu.make_async_remote_copy(
            src_ref=outb.at[p, pl.ds(first, end - first)], dst_ref=inbs[stage].at[p - low],
            send_sem=d_send.at[stage, p], recv_sem=d_recv.at[stage, p],
            device_id={"dp": partner(me, order[p])}, device_id_type=MESH,
        )

    def senders(stage):
        return [p for p in range(stages[stage][0], stages[stage][1]) if p != own]

    def reply(p):
        return exchange(backb, homeb, b_send, b_recv, p, p)

    others = [p for p in range(n) if p != own]
    for stage in range(begun):
        for p in senders(stage):
            dispatch(stage, p).start()
    for stage, (low, high, first, end) in enumerate(stages):
        if low <= own < high:
            inbs[stage][own - low] = outb[own, first:end]

    load_outw.wait()
    for lower in range(0, outw.shape[1], LANES):
        outw_t[lower:lower + LANES, :] = outw[:, lower:lower + LANES].T
        gain_t[lower:lower + LANES, :] = jnp.broadcast_to(
            gain_ref[lower // LANES:lower // LANES + 1, :], (LANES, LANES)
        ).T

    row = lax.broadcasted_iota(jnp.int32, (width, width), 0)
    col = lax.broadcasted_iota(jnp.int32, (width, width), 1)
    spread = jnp.where(
        row == jnp.where(col < rows, 2 * col, 2 * (col - rows) + 1), 1.0, 0.0
    ).astype(BF16)
    gathered = jnp.where(
        col == jnp.where(row < rows, 2 * row, 2 * (row - rows) + 1), 1.0, 0.0
    ).astype(BF16)
    low_half = lax.broadcasted_iota(jnp.int32, (rows, LANES), 1) < WIN

    for stage in range(begun, len(stages)):
        for p in senders(stage):
            dispatch(stage, p).start()
    load_qkv.wait()
    for p in senders(0):
        dispatch(0, p).wait()

    def window_in(k, upto):
        at = index_s[CHOSEN, k]
        p, j = at // cap, lax.rem(at, cap)
        found = None
        for (low, high, first, end), landed in zip(stages[:upto], inbs[:upto]):
            part_p = jnp.clip(p, low, high - 1) - low
            part_j = jnp.clip(j, first, end - 1) - first
            value = landed[part_p, part_j].astype(F32)
            if found is None:
                found = value
            else:
                here = (p >= low) & (p < high) & (j >= first) & (j < end)
                found = jnp.where(here, value, found)
        return found

    def unpack(c, upto):
        for p in range(PAIRS):
            first = window_in((c * PAIRS + p) * 2, upto)
            second = window_in((c * PAIRS + p) * 2 + 1, upto)
            even = jnp.where(low_half, first, pltpu.roll(second, WIN, 1))
            odd = jnp.where(low_half, pltpu.roll(first, WIN, 1), second)
            halves = jnp.concatenate([even, odd], axis=0).astype(BF16)
            block = jnp.dot(spread, halves, preferred_element_type=F32).astype(BF16)
            gath[z, c, :, p * LANES:(p + 1) * LANES] = block

    def ag_copy(c, o, step, send):
        return pltpu.make_async_remote_copy(
            src_ref=gath.at[o, c], dst_ref=gath.at[o, c],
            send_sem=send.at[c, o], recv_sem=ag_recv.at[c, o],
            device_id={"mp": z + step}, device_id_type=MESH,
        )

    def ag_own(c):
        @pl.when(z < m - 1)
        def _():
            ag_copy(c, z, 1, ag_right).start()

        @pl.when(z > 0)
        def _():
            ag_copy(c, z, -1, ag_left).start()

    def ag_step(c, t):
        @pl.when(z >= t)
        def _():
            ag_copy(c, z - t, -1, ag_left).wait_recv()

            @pl.when(z < m - 1)
            def _():
                ag_copy(c, z - t, 1, ag_right).start()

        @pl.when(z + t < m)
        def _():
            ag_copy(c, z + t, 1, ag_right).wait_recv()

            @pl.when(z > 0)
            def _():
                ag_copy(c, z + t, -1, ag_left).start()

    def rs_copy(c, s, step, landing, recv):
        return pltpu.make_async_remote_copy(
            src_ref=part.at[c, s], dst_ref=landing.at[c, s],
            send_sem=rs_send.at[c, s], recv_sem=recv.at[c, s],
            device_id={"mp": z + step}, device_id_type=MESH,
        )

    def rs_stage(c, k):
        @pl.when(z == k)
        def _():
            def step(i, _):
                s = m - 1 - i
                if k > 0:
                    rs_copy(c, s, -1, from_left, rs_left).wait_recv()
                    part[c, s] = (part[c, s].astype(F32) + from_left[c, s].astype(F32)).astype(BF16)
                rs_copy(c, s, 1, from_left, rs_left).start()
                return 0

            lax.fori_loop(0, m - 1 - k, step, 0)

        @pl.when(z == m - 1 - k)
        def _():
            def step(s, _):
                if k > 0:
                    rs_copy(c, s, 1, from_right, rs_right).wait_recv()
                    part[c, s] = (part[c, s].astype(F32) + from_right[c, s].astype(F32)).astype(BF16)
                rs_copy(c, s, -1, from_right, rs_right).start()
                return 0

            lax.fori_loop(0, m - 1 - k, step, 0)

    def rs_final(c):
        total[...] = part[c, z].astype(F32)

        @pl.when(z > 0)
        def _():
            rs_copy(c, z, -1, from_left, rs_left).wait_recv()
            total[...] += from_left[c, z].astype(F32)

        @pl.when(z < m - 1)
        def _():
            rs_copy(c, z, 1, from_right, rs_right).wait_recv()
            total[...] += from_right[c, z].astype(F32)

        block = (total[...] + gath[z, c].astype(F32)).astype(BF16)
        halves = jnp.dot(gathered, block, preferred_element_type=F32)
        for p in range(PAIRS):
            even = halves[:rows, p * LANES:(p + 1) * LANES]
            odd = halves[rows:, p * LANES:(p + 1) * LANES]
            k = (c * PAIRS + p) * 2
            done[k] = jnp.where(low_half, even, pltpu.roll(odd, WIN, 1)).astype(BF16)
            done[k + 1] = jnp.where(low_half, pltpu.roll(even, WIN, 1), odd).astype(BF16)

    def project(c):
        full = gath[:, c].reshape(m * width, PAIRS * LANES).astype(F32)
        mean_square = jnp.mean(full * full, axis=0, keepdims=True)
        gain = jnp.concatenate([gain_t[...]] * PAIRS, axis=1)
        normed = (full * lax.rsqrt(mean_square + epsilon) * gain).astype(BF16)
        proj[...] = jnp.dot(qkv_t[...], normed, preferred_element_type=F32).astype(BF16)

    first_window = iota((WIN, LANES), 1) < WIN

    def attend(p):
        lanes = slice(p * LANES, (p + 1) * LANES)
        scores = []
        for h in range(heads_here):
            base = h * 3 * HEAD_DIM
            queries = proj[base:base + HEAD_DIM, lanes]
            key_vecs = proj[base + HEAD_DIM:base + 2 * HEAD_DIM, lanes]
            both = lax.dot_general(
                key_vecs, queries, (((0,), (0,)), ((), ())), preferred_element_type=F32
            )
            scores.append(jnp.where(first_window, both[:WIN], both[WIN:]))
        scores = jnp.concatenate(scores, axis=1) * (HEAD_DIM ** (-0.5) * LOG2E)
        weights = jnp.exp2(scores - jnp.max(scores, axis=0, keepdims=True))
        probs = weights * (1.0 / jnp.sum(weights, axis=0, keepdims=True))
        for h in range(heads_here):
            base = h * 3 * HEAD_DIM
            value_vecs = proj[base + 2 * HEAD_DIM:base + 3 * HEAD_DIM, lanes]
            mine = probs[:, h * LANES:(h + 1) * LANES]
            spread_probs = jnp.concatenate(
                [jnp.where(first_window, mine, 0.0), jnp.where(first_window, 0.0, mine)], axis=0
            ).astype(BF16)
            heads[h * HEAD_DIM:(h + 1) * HEAD_DIM, lanes] = jnp.dot(
                value_vecs, spread_probs, preferred_element_type=F32
            ).astype(BF16)

    def output(c):
        for s in range(m):
            part[c, s] = jnp.dot(
                outw_t[s * width:(s + 1) * width, :], heads[...], preferred_element_type=F32
            ).astype(BF16)

    chunk_win = 2 * PAIRS
    needed = [stages_needed(n, cap, c) for c in range(chunks)]

    def own_chunk(c):
        for stage in range(1, len(stages)):
            @pl.when(c == sum(upto <= stage for upto in needed))
            def _():
                for p in senders(stage):
                    dispatch(stage, p).wait()

        for upto in sorted(set(needed)):
            low = needed.index(upto)

            @pl.when(jnp.logical_and(c >= low, c < low + needed.count(upto)))
            def _():
                unpack(c, upto)

        ag_own(c)

    def ready(p):
        return (min(ENC_WIN, cap * (p + 1)) - 1) // chunk_win

    def answer(p):
        for j in range(cap):
            backb[p, j] = done[index_s[BACK, p * cap + j]]
        if p != own:
            reply(p).start()

    def finish(c):
        rs_final(c)
        for p in range(n):
            if ready(p) < chunks - 1:
                pl.when(c == ready(p))(functools.partial(answer, p))


    def within(c, act):
        @pl.when(jnp.logical_and(c >= 0, c < chunks))
        def _():
            act(c)

    def compute(c):
        project(c)
        for p in range(PAIRS):
            attend(p)
        output(c)

    def turn(i, _):
        c = i - (m - 1)
        for t in range(m - 1, 0, -1):
            within(c + m - 1 - t, lambda at, t=t: ag_step(at, t))
        within(c + m - 1, own_chunk)
        within(c, compute)
        within(c, lambda at: rs_stage(at, 0))
        for k in range(1, m - 1):
            within(c - k, lambda at, k=k: rs_stage(at, k))
        within(c - (m - 1), finish)
        return 0

    lax.fori_loop(0, chunks + 2 * (m - 1), turn, 0)

    for p in range(n):
        if ready(p) == chunks - 1:
            answer(p)
    homeb[own] = backb[own]
    homeb[n] = jnp.zeros_like(homeb[n])

    def sent(c, _):
        def each(o, _):
            @pl.when(jnp.logical_and(z < m - 1, o <= z))
            def _():
                ag_copy(c, o, 1, ag_right).wait_send()

            @pl.when(jnp.logical_and(z > 0, o >= z))
            def _():
                ag_copy(c, o, -1, ag_left).wait_send()

            @pl.when(o > z)
            def _():
                rs_copy(c, o, 1, from_left, rs_left).wait_send()

            @pl.when(o < z)
            def _():
                rs_copy(c, o, -1, from_right, rs_right).wait_send()

            return 0

        return lax.fori_loop(0, m, each, 0)

    lax.fori_loop(0, chunks, sent, 0)
    for p in others:
        reply(p).wait()

    def place_home(s, _):
        at = index_s[SLOT, s]
        out_ref[s] = homeb[at // cap, lax.rem(at, cap)]
        return 0

    lax.fori_loop(0, home_win, place_home, 0)


def body(patches, norm_gain, qkv_weight, out_weight, window_plan):
    n = lax.axis_size("dp")
    m = lax.axis_size("mp")
    home_win, row_width = patches.shape
    rows = row_width // LANES
    width = 2 * rows
    full_width = width * m
    cap = (home_win + n - 1) // n
    chunks = ENC_WIN // (2 * PAIRS)
    cols = PAIRS * LANES
    stages = arrival_stages(n, cap)

    hbm = pl.BlockSpec(memory_space=pl.ANY)
    vmem = pl.BlockSpec(memory_space=pltpu.VMEM)
    dma = pltpu.SemaphoreType.DMA
    result = pl.pallas_call(
        functools.partial(kernel, n, m, cap),
        out_shape=jax.ShapeDtypeStruct((home_win, rows, LANES), BF16),
        in_specs=[vmem] * 3 + [hbm] * 2,
        out_specs=vmem,
        scratch_shapes=[
            pltpu.VMEM((8, LANES), jnp.int32),
            pltpu.SMEM((8, LANES), jnp.int32),
            pltpu.VMEM(out_weight.shape, BF16),
            pltpu.VMEM((full_width, LANES), F32),
            pltpu.VMEM((n, cap, rows, LANES), BF16),
            [
                pltpu.VMEM((high - low, end - first, rows, LANES), BF16)
                for low, high, first, end in stages
            ],
            pltpu.VMEM((m, chunks, width, cols), BF16),
            pltpu.VMEM((qkv_weight.shape[1], full_width), BF16),
            pltpu.VMEM((full_width, out_weight.shape[0]), BF16),
            pltpu.VMEM((qkv_weight.shape[1], cols), BF16),
            pltpu.VMEM((out_weight.shape[0], cols), BF16),
            pltpu.VMEM((chunks, m, width, cols), BF16),
            pltpu.VMEM((chunks, m, width, cols), BF16),
            pltpu.VMEM((chunks, m, width, cols), BF16),
            pltpu.VMEM((width, cols), F32),
            pltpu.VMEM((ENC_WIN, rows, LANES), BF16),
            pltpu.VMEM((n, cap, rows, LANES), BF16),
            pltpu.VMEM((n + 1, cap, rows, LANES), BF16),
            dma, dma((2,)), dma((len(stages), n)), dma((len(stages), n)), dma((n,)), dma((n,)),
            dma((chunks, m)), dma((chunks, m)), dma((chunks, m)),
            dma((chunks, m)), dma((chunks, m)), dma((chunks, m)),
        ],
        compiler_params=pltpu.CompilerParams(
            collective_id=0, has_side_effects=True, vmem_limit_bytes=56 * 1024 * 1024
        ),
    )(
        window_plan, patches.reshape(home_win, rows, LANES), norm_gain.reshape(-1, LANES),
        qkv_weight.T, out_weight,
    )
    return result.reshape(home_win, row_width)


def solution(mesh):
    return jax.shard_map(
        body,
        mesh=mesh,
        in_specs=(P("dp", "mp"), P(), P(None, "mp"), P("mp", None), P()),
        out_specs=P("dp", "mp"),
        check_vma=False,
    )
```

```python
import functools

import jax
import jax.numpy as jnp
from jax import lax
from jax.experimental import pallas as pl
from jax.experimental.pallas import tpu as pltpu
from jax.sharding import PartitionSpec as P

HEAD_DIM = 80
WIN = 64
ENC_WIN = 16
LANES = 128
PAIRS = 1
TILE = 8

LOG2E = 1.4426950408889634
epsilon = 1e-06
MESH = pl.DeviceIdType.MESH
F32 = jnp.float32
BF16 = jnp.bfloat16


SOURCE, CHOSEN, BACK, SLOT = range(4)


def early_positions(n, cap):
    return n - (ENC_WIN - 2 * PAIRS) // cap


def arrival_stages(n, cap):
    early, reach = early_positions(n, cap), min(cap, 2 * PAIRS)
    stages = [(0, early, 0, reach), (0, early, reach, cap)]
    stages += [(early, early + 1, 0, cap), (early + 1, n, 0, cap)]
    return [part for part in stages if part[0] < part[1] and part[2] < part[3]]


def early_stages(n, cap):
    return sum(part[0] == 0 for part in arrival_stages(n, cap))


def stages_needed(n, cap, c):
    last = (c + 1) * 2 * PAIRS - 1
    positions = n - (ENC_WIN - 1 - last) // cap
    return max(
        at + 1
        for at, (low, _, first, _) in enumerate(arrival_stages(n, cap))
        if low < positions and first <= last
    )


def position_order(n, cap):
    far = list(range(n - 2, 1, -2)) + list(range(n - 1, 2, -2))
    split = early_positions(n, cap) - 2
    return far[:split] + [1, 0] + far[split:]


def position_of(flip, n, cap):
    split = early_positions(n, cap) - 2
    at = jnp.where(flip % 2 == 0, (n - 2 - flip) // 2, n // 2 - 1 + (n - 1 - flip) // 2)
    at = jnp.where(at >= split, at + 2, at)
    return jnp.where(flip == 1, split, jnp.where(flip == 0, split + 1, at))


def partner(me, flip):
    other, bit = me, 1
    while bit <= flip:
        if (flip // bit) % 2:
            other = other + bit * (1 - 2 * ((me // bit) % 2))
        bit *= 2
    return other


def iota(shape, axis):
    return lax.broadcasted_iota(jnp.int32, shape, axis)


def plan_indices(n, cap, me, plan_ref, index_v):
    plan = plan_ref[...]
    index_v[...] = jnp.zeros_like(index_v)
    slots = plan.shape[1]
    mine = plan_ref[pl.ds(me, 1), :]
    same = iota((slots, slots), 0) == iota((slots, slots), 1)
    turned = jnp.sum(jnp.where(same, mine, 0), axis=1, keepdims=True)
    earlier = (turned == mine) & (iota((slots, slots), 1) < iota((slots, slots), 0))
    ordinal = jnp.sum(earlier.astype(jnp.int32), axis=1, keepdims=True)
    place = jnp.where(turned >= 0, position_of(turned ^ me, n, cap) * cap + ordinal, n * cap)
    grid = (slots, n * cap)
    source = jnp.sum(
        jnp.where(place == iota(grid, 1), iota(grid, 0), 0), axis=0, keepdims=True
    )
    index_v[SOURCE:SOURCE + 1, :n * cap] = jnp.clip(source, 0, slots - 1)
    index_v[SLOT:SLOT + 1, :slots] = jnp.minimum(
        jnp.sum(jnp.where(same, place, 0), axis=0, keepdims=True), n * cap
    )

    counts = jnp.sum((plan == me).astype(jnp.int32), axis=1, keepdims=True)
    square = (n, n)
    counts_row = jnp.sum(
        jnp.where(iota(square, 0) == iota(square, 1), counts, 0), axis=0, keepdims=True
    )
    at_col = position_of(iota((n, 1), 0) ^ me, n, cap)
    at_row = position_of(iota((1, n), 1) ^ me, n, cap)
    offsets = jnp.sum(jnp.where(at_row < at_col, counts_row, 0), axis=1, keepdims=True)
    j = iota((n, ENC_WIN), 1) - offsets
    chosen = jnp.sum(
        jnp.where((j >= 0) & (j < counts), at_col * cap + j, 0), axis=0, keepdims=True
    )
    index_v[CHOSEN:CHOSEN + 1, :ENC_WIN] = jnp.clip(chosen, 0, n * cap - 1)
    q = iota((n, n * cap), 1)
    back = jnp.sum(
        jnp.where(q // cap == at_col, offsets + q % cap, 0), axis=0, keepdims=True
    )
    index_v[BACK:BACK + 1, :n * cap] = jnp.clip(back, 0, ENC_WIN - 1)


def kernel(
    n, m, cap,
    plan_ref, x_ref, gain_ref, qkv_ref, outw_ref,
    out_ref,
    index_v, index_s, flat, outw, gain_t, outb, inbs, gath, qkv_t, outw_t, proj, heads, part, from_left, from_right, total, done, backb, homeb,
    i_sem, w_sem, d_send, d_recv, b_send, b_recv, ag_recv, ag_right, ag_left, rs_send, rs_left, rs_right,
):
    me = lax.axis_index("dp")
    z = lax.axis_index("mp")
    rows = x_ref.shape[1]
    home_win = x_ref.shape[0] * TILE
    width = 2 * rows
    chunks = gath.shape[1]
    heads_here = qkv_ref.shape[0] // (3 * HEAD_DIM)

    order = position_order(n, cap)

    load_qkv = pltpu.make_async_copy(qkv_ref, qkv_t, w_sem.at[0])
    load_outw = pltpu.make_async_copy(outw_ref, outw, w_sem.at[1])
    load_qkv.start()
    load_outw.start()

    barrier = pltpu.get_barrier_semaphore()

    for d in range(1, n):
        pl.semaphore_signal(
            barrier, inc=1, device_id={"dp": partner(me, d)}, device_id_type=MESH
        )

    @pl.when(z > 0)
    def _():
        pl.semaphore_signal(barrier, inc=1, device_id={"mp": z - 1}, device_id_type=MESH)

    @pl.when(z < m - 1)
    def _():
        pl.semaphore_signal(barrier, inc=1, device_id={"mp": z + 1}, device_id_type=MESH)

    plan_indices(n, cap, me, plan_ref, index_v)
    load_index = pltpu.make_async_copy(index_v, index_s, i_sem)
    load_index.start()

    def widen(g, _):
        at = pl.ds(pl.multiple_of(g * (rows * TILE), rows * TILE), rows * TILE)
        flat[at, :] = x_ref[g].reshape(rows * TILE, LANES).astype(F32)
        return 0

    lax.fori_loop(0, home_win // TILE, widen, 0)
    load_index.wait()

    def window_rows(s):
        return pl.ds((s // TILE) * (rows * TILE) + lax.rem(s, TILE), rows, stride=TILE)

    for p in range(n):
        for j in range(cap):
            outb[p, j] = flat[window_rows(index_s[SOURCE, p * cap + j]), :].astype(BF16)

    ends = (z == 0).astype(jnp.int32) + (z == m - 1).astype(jnp.int32)
    pl.semaphore_wait(barrier, n + 1 - ends)

    own = order.index(0)

    own = order.index(0)
    stages = arrival_stages(n, cap)
    begun = early_stages(n, cap)

    def exchange(src, dst, send, recv, p, at):
        return pltpu.make_async_remote_copy(
            src_ref=src.at[p], dst_ref=dst.at[at], send_sem=send.at[p], recv_sem=recv.at[p],
            device_id={"dp": partner(me, order[p])}, device_id_type=MESH,
        )

    def dispatch(stage, p):
        low, _, first, end = stages[stage]
        return pltpu.make_async_remote_copy(
            src_ref=outb.at[p, pl.ds(first, end - first)], dst_ref=inbs[stage].at[p - low],
            send_sem=d_send.at[stage, p], recv_sem=d_recv.at[stage, p],
            device_id={"dp": partner(me, order[p])}, device_id_type=MESH,
        )

    def senders(stage):
        return [p for p in range(stages[stage][0], stages[stage][1]) if p != own]

    def reply(p):
        return exchange(backb, homeb, b_send, b_recv, p, p)

    others = [p for p in range(n) if p != own]
    for stage in range(begun):
        for p in senders(stage):
            dispatch(stage, p).start()
    for stage, (low, high, first, end) in enumerate(stages):
        if low <= own < high:
            inbs[stage][own - low] = outb[own, first:end]

    load_outw.wait()
    for lower in range(0, outw.shape[1], LANES):
        outw_t[lower:lower + LANES, :] = outw[:, lower:lower + LANES].T
        gain_t[lower:lower + LANES, :] = jnp.broadcast_to(
            gain_ref[lower // LANES:lower // LANES + 1, :], (LANES, LANES)
        ).T

    row = lax.broadcasted_iota(jnp.int32, (width, width), 0)
    col = lax.broadcasted_iota(jnp.int32, (width, width), 1)
    spread = jnp.where(
        row == jnp.where(col < rows, 2 * col, 2 * (col - rows) + 1), 1.0, 0.0
    ).astype(BF16)
    gathered = jnp.where(
        col == jnp.where(row < rows, 2 * row, 2 * (row - rows) + 1), 1.0, 0.0
    ).astype(BF16)
    low_half = lax.broadcasted_iota(jnp.int32, (rows, LANES), 1) < WIN

    for stage in range(begun, len(stages)):
        for p in senders(stage):
            dispatch(stage, p).start()
    load_qkv.wait()
    for p in senders(0):
        dispatch(0, p).wait()

    def window_in(k, upto):
        at = index_s[CHOSEN, k]
        p, j = at // cap, lax.rem(at, cap)
        found = None
        for (low, high, first, end), landed in zip(stages[:upto], inbs[:upto]):
            part_p = jnp.clip(p, low, high - 1) - low
            part_j = jnp.clip(j, first, end - 1) - first
            value = landed[part_p, part_j].astype(F32)
            if found is None:
                found = value
            else:
                here = (p >= low) & (p < high) & (j >= first) & (j < end)
                found = jnp.where(here, value, found)
        return found

    def unpack(c, upto):
        for p in range(PAIRS):
            first = window_in((c * PAIRS + p) * 2, upto)
            second = window_in((c * PAIRS + p) * 2 + 1, upto)
            even = jnp.where(low_half, first, pltpu.roll(second, WIN, 1))
            odd = jnp.where(low_half, pltpu.roll(first, WIN, 1), second)
            halves = jnp.concatenate([even, odd], axis=0).astype(BF16)
            block = jnp.dot(spread, halves, preferred_element_type=F32).astype(BF16)
            gath[z, c, :, p * LANES:(p + 1) * LANES] = block

    def ag_copy(c, o, step, send):
        return pltpu.make_async_remote_copy(
            src_ref=gath.at[o, c], dst_ref=gath.at[o, c],
            send_sem=send.at[c, o], recv_sem=ag_recv.at[c, o],
            device_id={"mp": z + step}, device_id_type=MESH,
        )

    def ag_own(c):
        @pl.when(z < m - 1)
        def _():
            ag_copy(c, z, 1, ag_right).start()

        @pl.when(z > 0)
        def _():
            ag_copy(c, z, -1, ag_left).start()

    def ag_step(c, t):
        @pl.when(z >= t)
        def _():
            ag_copy(c, z - t, -1, ag_left).wait_recv()

            @pl.when(z < m - 1)
            def _():
                ag_copy(c, z - t, 1, ag_right).start()

        @pl.when(z + t < m)
        def _():
            ag_copy(c, z + t, 1, ag_right).wait_recv()

            @pl.when(z > 0)
            def _():
                ag_copy(c, z + t, -1, ag_left).start()

    def rs_copy(c, s, step, landing, recv):
        return pltpu.make_async_remote_copy(
            src_ref=part.at[c, s], dst_ref=landing.at[c, s],
            send_sem=rs_send.at[c, s], recv_sem=recv.at[c, s],
            device_id={"mp": z + step}, device_id_type=MESH,
        )

    def rs_stage(c, k):
        @pl.when(z == k)
        def _():
            def step(i, _):
                s = m - 1 - i
                if k > 0:
                    rs_copy(c, s, -1, from_left, rs_left).wait_recv()
                    part[c, s] = (part[c, s].astype(F32) + from_left[c, s].astype(F32)).astype(BF16)
                rs_copy(c, s, 1, from_left, rs_left).start()
                return 0

            lax.fori_loop(0, m - 1 - k, step, 0)

        @pl.when(z == m - 1 - k)
        def _():
            def step(s, _):
                if k > 0:
                    rs_copy(c, s, 1, from_right, rs_right).wait_recv()
                    part[c, s] = (part[c, s].astype(F32) + from_right[c, s].astype(F32)).astype(BF16)
                rs_copy(c, s, -1, from_right, rs_right).start()
                return 0

            lax.fori_loop(0, m - 1 - k, step, 0)

    def rs_final(c):
        total[...] = part[c, z].astype(F32)

        @pl.when(z > 0)
        def _():
            rs_copy(c, z, -1, from_left, rs_left).wait_recv()
            total[...] += from_left[c, z].astype(F32)

        @pl.when(z < m - 1)
        def _():
            rs_copy(c, z, 1, from_right, rs_right).wait_recv()
            total[...] += from_right[c, z].astype(F32)

        block = (total[...] + gath[z, c].astype(F32)).astype(BF16)
        halves = jnp.dot(gathered, block, preferred_element_type=F32)
        for p in range(PAIRS):
            even = halves[:rows, p * LANES:(p + 1) * LANES]
            odd = halves[rows:, p * LANES:(p + 1) * LANES]
            k = (c * PAIRS + p) * 2
            done[k] = jnp.where(low_half, even, pltpu.roll(odd, WIN, 1)).astype(BF16)
            done[k + 1] = jnp.where(low_half, pltpu.roll(even, WIN, 1), odd).astype(BF16)

    def project(c):
        full = gath[:, c].reshape(m * width, PAIRS * LANES).astype(F32)
        mean_square = jnp.mean(full * full, axis=0, keepdims=True)
        gain = jnp.concatenate([gain_t[...]] * PAIRS, axis=1)
        normed = (full * lax.rsqrt(mean_square + epsilon) * gain).astype(BF16)
        proj[...] = jnp.dot(qkv_t[...], normed, preferred_element_type=F32).astype(BF16)

    first_window = iota((WIN, LANES), 1) < WIN

    def attend(p):
        lanes = slice(p * LANES, (p + 1) * LANES)
        scores = []
        for h in range(heads_here):
            base = h * 3 * HEAD_DIM
            queries = proj[base:base + HEAD_DIM, lanes]
            key_vecs = proj[base + HEAD_DIM:base + 2 * HEAD_DIM, lanes]
            both = lax.dot_general(
                key_vecs, queries, (((0,), (0,)), ((), ())), preferred_element_type=F32
            )
            scores.append(jnp.where(first_window, both[:WIN], both[WIN:]))
        scores = jnp.concatenate(scores, axis=1) * (HEAD_DIM ** (-0.5) * LOG2E)
        weights = jnp.exp2(scores - jnp.max(scores, axis=0, keepdims=True))
        probs = weights * (1.0 / jnp.sum(weights, axis=0, keepdims=True))
        for h in range(heads_here):
            base = h * 3 * HEAD_DIM
            value_vecs = proj[base + 2 * HEAD_DIM:base + 3 * HEAD_DIM, lanes]
            mine = probs[:, h * LANES:(h + 1) * LANES]
            spread_probs = jnp.concatenate(
                [jnp.where(first_window, mine, 0.0), jnp.where(first_window, 0.0, mine)], axis=0
            ).astype(BF16)
            heads[h * HEAD_DIM:(h + 1) * HEAD_DIM, lanes] = jnp.dot(
                value_vecs, spread_probs, preferred_element_type=F32
            ).astype(BF16)

    def output(c):
        for s in range(m):
            part[c, s] = jnp.dot(
                outw_t[s * width:(s + 1) * width, :], heads[...], preferred_element_type=F32
            ).astype(BF16)

    chunk_win = 2 * PAIRS
    needed = [stages_needed(n, cap, c) for c in range(chunks)]

    def own_chunk(c):
        for stage in range(1, len(stages)):
            @pl.when(c == sum(upto <= stage for upto in needed))
            def _():
                for p in senders(stage):
                    dispatch(stage, p).wait()

        for upto in sorted(set(needed)):
            low = needed.index(upto)

            @pl.when(jnp.logical_and(c >= low, c < low + needed.count(upto)))
            def _():
                unpack(c, upto)

        ag_own(c)

    def ready(p):
        return (min(ENC_WIN, cap * (p + 1)) - 1) // chunk_win

    def answer(p):
        for j in range(cap):
            backb[p, j] = done[index_s[BACK, p * cap + j]]
        if p != own:
            reply(p).start()

    def finish(c):
        rs_final(c)
        for p in range(n):
            if ready(p) < chunks - 1:
                pl.when(c == ready(p))(functools.partial(answer, p))


    def within(c, act):
        @pl.when(jnp.logical_and(c >= 0, c < chunks))
        def _():
            act(c)

    def compute(c):
        project(c)
        for p in range(PAIRS):
            attend(p)
        output(c)

    def turn(i, _):
        c = i - (m - 1)
        for t in range(m - 1, 0, -1):
            within(c + m - 1 - t, lambda at, t=t: ag_step(at, t))
        within(c + m - 1, own_chunk)
        within(c, compute)
        within(c, lambda at: rs_stage(at, 0))
        for k in range(1, m - 1):
            within(c - k, lambda at, k=k: rs_stage(at, k))
        within(c - (m - 1), finish)
        return 0

    lax.fori_loop(0, chunks + 2 * (m - 1), turn, 0)

    for p in range(n):
        if ready(p) == chunks - 1:
            answer(p)
    homeb[own] = backb[own]
    homeb[n] = jnp.zeros_like(homeb[n])

    def sent(c, _):
        def each(o, _):
            @pl.when(jnp.logical_and(z < m - 1, o <= z))
            def _():
                ag_copy(c, o, 1, ag_right).wait_send()

            @pl.when(jnp.logical_and(z > 0, o >= z))
            def _():
                ag_copy(c, o, -1, ag_left).wait_send()

            @pl.when(o > z)
            def _():
                rs_copy(c, o, 1, from_left, rs_left).wait_send()

            @pl.when(o < z)
            def _():
                rs_copy(c, o, -1, from_right, rs_right).wait_send()

            return 0

        return lax.fori_loop(0, m, each, 0)

    lax.fori_loop(0, chunks, sent, 0)
    for p in others:
        reply(p).wait()

    def place_home(s, _):
        at = index_s[SLOT, s]
        flat[window_rows(s), :] = homeb[at // cap, lax.rem(at, cap)].astype(F32)
        return 0

    lax.fori_loop(0, home_win, place_home, 0)

    def narrow(g, _):
        at = pl.ds(pl.multiple_of(g * (rows * TILE), rows * TILE), rows * TILE)
        out_ref[g] = flat[at, :].astype(BF16).reshape(rows, TILE, LANES)
        return 0

    lax.fori_loop(0, home_win // TILE, narrow, 0)


def body(patches, norm_gain, qkv_weight, out_weight, window_plan):
    n = lax.axis_size("dp")
    m = lax.axis_size("mp")
    home_win, row_width = patches.shape
    rows = row_width // LANES
    width = 2 * rows
    full_width = width * m
    cap = (home_win + n - 1) // n
    chunks = ENC_WIN // (2 * PAIRS)
    cols = PAIRS * LANES
    stages = arrival_stages(n, cap)

    tiles = jnp.transpose(
        patches.reshape(home_win // TILE, TILE, rows, LANES), (0, 2, 1, 3)
    )
    hbm = pl.BlockSpec(memory_space=pl.ANY)
    vmem = pl.BlockSpec(memory_space=pltpu.VMEM)
    dma = pltpu.SemaphoreType.DMA
    result = pl.pallas_call(
        functools.partial(kernel, n, m, cap),
        out_shape=jax.ShapeDtypeStruct(tiles.shape, BF16),
        in_specs=[vmem] * 3 + [hbm] * 2,
        out_specs=vmem,
        scratch_shapes=[
            pltpu.VMEM((8, LANES), jnp.int32),
            pltpu.SMEM((8, LANES), jnp.int32),
            pltpu.VMEM((home_win * rows, LANES), F32),
            pltpu.VMEM(out_weight.shape, BF16),
            pltpu.VMEM((full_width, LANES), F32),
            pltpu.VMEM((n, cap, rows, LANES), BF16),
            [
                pltpu.VMEM((high - low, end - first, rows, LANES), BF16)
                for low, high, first, end in stages
            ],
            pltpu.VMEM((m, chunks, width, cols), BF16),
            pltpu.VMEM((qkv_weight.shape[1], full_width), BF16),
            pltpu.VMEM((full_width, out_weight.shape[0]), BF16),
            pltpu.VMEM((qkv_weight.shape[1], cols), BF16),
            pltpu.VMEM((out_weight.shape[0], cols), BF16),
            pltpu.VMEM((chunks, m, width, cols), BF16),
            pltpu.VMEM((chunks, m, width, cols), BF16),
            pltpu.VMEM((chunks, m, width, cols), BF16),
            pltpu.VMEM((width, cols), F32),
            pltpu.VMEM((ENC_WIN, rows, LANES), BF16),
            pltpu.VMEM((n, cap, rows, LANES), BF16),
            pltpu.VMEM((n + 1, cap, rows, LANES), BF16),
            dma, dma((2,)), dma((len(stages), n)), dma((len(stages), n)), dma((n,)), dma((n,)),
            dma((chunks, m)), dma((chunks, m)), dma((chunks, m)),
            dma((chunks, m)), dma((chunks, m)), dma((chunks, m)),
        ],
        compiler_params=pltpu.CompilerParams(
            collective_id=0, has_side_effects=True, vmem_limit_bytes=56 * 1024 * 1024
        ),
    )(
        window_plan, tiles, norm_gain.reshape(-1, LANES),
        qkv_weight.T, out_weight,
    )
    return jnp.transpose(result, (0, 2, 1, 3)).reshape(home_win, row_width)


def solution(mesh):
    return jax.shard_map(
        body,
        mesh=mesh,
        in_specs=(P("dp", "mp"), P(), P(None, "mp"), P("mp", None), P()),
        out_specs=P("dp", "mp"),
        check_vma=False,
    )
```

```python
import functools

import jax
import jax.numpy as jnp
from jax import lax
from jax.experimental import pallas as pl
from jax.experimental.pallas import tpu as pltpu
from jax.sharding import PartitionSpec as P

HEAD_DIM = 80
WIN = 64
ENC_WIN = 16
LANES = 128
PAIRS = 1
TILE = 8

LOG2E = 1.4426950408889634
epsilon = 1e-06
MESH = pl.DeviceIdType.MESH
F32 = jnp.float32
BF16 = jnp.bfloat16


SOURCE, CHOSEN, BACK, SLOT = range(4)


def early_positions(n, cap):
    return n - (ENC_WIN - 2 * PAIRS) // cap


def arrival_stages(n, cap):
    early, reach = early_positions(n, cap), min(cap, 2 * PAIRS)
    stages = [(0, early, 0, reach), (0, early, reach, cap)]
    stages += [(early, early + 1, 0, cap), (early + 1, n, 0, cap)]
    return [part for part in stages if part[0] < part[1] and part[2] < part[3]]


def early_stages(n, cap):
    return sum(part[0] == 0 for part in arrival_stages(n, cap))


def stages_needed(n, cap, c):
    last = (c + 1) * 2 * PAIRS - 1
    positions = n - (ENC_WIN - 1 - last) // cap
    return max(
        at + 1
        for at, (low, _, first, _) in enumerate(arrival_stages(n, cap))
        if low < positions and first <= last
    )


def position_order(n, cap):
    far = list(range(n - 2, 1, -2)) + list(range(n - 1, 2, -2))
    split = early_positions(n, cap) - 2
    return far[:split] + [1, 0] + far[split:]


def position_of(flip, n, cap):
    split = early_positions(n, cap) - 2
    at = jnp.where(flip % 2 == 0, (n - 2 - flip) // 2, n // 2 - 1 + (n - 1 - flip) // 2)
    at = jnp.where(at >= split, at + 2, at)
    return jnp.where(flip == 1, split, jnp.where(flip == 0, split + 1, at))


def partner(me, flip):
    other, bit = me, 1
    while bit <= flip:
        if (flip // bit) % 2:
            other = other + bit * (1 - 2 * ((me // bit) % 2))
        bit *= 2
    return other


def iota(shape, axis):
    return lax.broadcasted_iota(jnp.int32, shape, axis)


def plan_indices(n, cap, me, plan_ref, index_v):
    plan = plan_ref[...]
    index_v[...] = jnp.zeros_like(index_v)
    slots = plan.shape[1]
    mine = plan_ref[pl.ds(me, 1), :]
    same = iota((slots, slots), 0) == iota((slots, slots), 1)
    turned = jnp.sum(jnp.where(same, mine, 0), axis=1, keepdims=True)
    earlier = (turned == mine) & (iota((slots, slots), 1) < iota((slots, slots), 0))
    ordinal = jnp.sum(earlier.astype(jnp.int32), axis=1, keepdims=True)
    place = jnp.where(turned >= 0, position_of(turned ^ me, n, cap) * cap + ordinal, n * cap)
    grid = (slots, n * cap)
    source = jnp.sum(
        jnp.where(place == iota(grid, 1), iota(grid, 0), 0), axis=0, keepdims=True
    )
    index_v[SOURCE:SOURCE + 1, :n * cap] = jnp.clip(source, 0, slots - 1)
    index_v[SLOT:SLOT + 1, :slots] = jnp.minimum(
        jnp.sum(jnp.where(same, place, 0), axis=0, keepdims=True), n * cap
    )

    counts = jnp.sum((plan == me).astype(jnp.int32), axis=1, keepdims=True)
    square = (n, n)
    counts_row = jnp.sum(
        jnp.where(iota(square, 0) == iota(square, 1), counts, 0), axis=0, keepdims=True
    )
    at_col = position_of(iota((n, 1), 0) ^ me, n, cap)
    at_row = position_of(iota((1, n), 1) ^ me, n, cap)
    offsets = jnp.sum(jnp.where(at_row < at_col, counts_row, 0), axis=1, keepdims=True)
    j = iota((n, ENC_WIN), 1) - offsets
    chosen = jnp.sum(
        jnp.where((j >= 0) & (j < counts), at_col * cap + j, 0), axis=0, keepdims=True
    )
    index_v[CHOSEN:CHOSEN + 1, :ENC_WIN] = jnp.clip(chosen, 0, n * cap - 1)
    q = iota((n, n * cap), 1)
    back = jnp.sum(
        jnp.where(q // cap == at_col, offsets + q % cap, 0), axis=0, keepdims=True
    )
    index_v[BACK:BACK + 1, :n * cap] = jnp.clip(back, 0, ENC_WIN - 1)


def window_rows(s, rows):
    return pl.ds((s // TILE) * (rows * TILE) + lax.rem(s, TILE), rows, stride=TILE)


def kernel(
    n, m, cap,
    plan_ref, x_ref, gain_ref, qkv_ref, outw_ref,
    home_ref, slots_ref,
    index_v, index_s, flat, outw, gain_t, outb, inbs, gath, qkv_t, outw_t, proj, heads, part, from_left, from_right, total, done, backb, homeb,
    i_sem, w_sem, d_send, d_recv, b_send, b_recv, ag_recv, ag_right, ag_left, rs_send, rs_left, rs_right,
):
    me = lax.axis_index("dp")
    z = lax.axis_index("mp")
    rows = x_ref.shape[1]
    home_win = x_ref.shape[0] * TILE
    width = 2 * rows
    chunks = gath.shape[1]
    heads_here = qkv_ref.shape[0] // (3 * HEAD_DIM)

    order = position_order(n, cap)

    load_qkv = pltpu.make_async_copy(qkv_ref, qkv_t, w_sem.at[0])
    load_outw = pltpu.make_async_copy(outw_ref, outw, w_sem.at[1])
    load_qkv.start()
    load_outw.start()

    barrier = pltpu.get_barrier_semaphore()

    for d in range(1, n):
        pl.semaphore_signal(
            barrier, inc=1, device_id={"dp": partner(me, d)}, device_id_type=MESH
        )

    @pl.when(z > 0)
    def _():
        pl.semaphore_signal(barrier, inc=1, device_id={"mp": z - 1}, device_id_type=MESH)

    @pl.when(z < m - 1)
    def _():
        pl.semaphore_signal(barrier, inc=1, device_id={"mp": z + 1}, device_id_type=MESH)

    plan_indices(n, cap, me, plan_ref, index_v)
    load_index = pltpu.make_async_copy(index_v, index_s, i_sem)
    load_index.start()

    def widen(g, _):
        at = pl.ds(pl.multiple_of(g * (rows * TILE), rows * TILE), rows * TILE)
        flat[at, :] = x_ref[g].reshape(rows * TILE, LANES).astype(F32)
        return 0

    lax.fori_loop(0, home_win // TILE, widen, 0)
    load_index.wait()
    for p in range(n):
        for j in range(cap):
            outb[p, j] = flat[window_rows(index_s[SOURCE, p * cap + j], rows), :].astype(BF16)

    ends = (z == 0).astype(jnp.int32) + (z == m - 1).astype(jnp.int32)
    pl.semaphore_wait(barrier, n + 1 - ends)

    own = order.index(0)

    own = order.index(0)
    stages = arrival_stages(n, cap)
    begun = early_stages(n, cap)

    def exchange(src, dst, send, recv, p, at):
        return pltpu.make_async_remote_copy(
            src_ref=src.at[p], dst_ref=dst.at[at], send_sem=send.at[p], recv_sem=recv.at[p],
            device_id={"dp": partner(me, order[p])}, device_id_type=MESH,
        )

    def dispatch(stage, p):
        low, _, first, end = stages[stage]
        return pltpu.make_async_remote_copy(
            src_ref=outb.at[p, pl.ds(first, end - first)], dst_ref=inbs[stage].at[p - low],
            send_sem=d_send.at[stage, p], recv_sem=d_recv.at[stage, p],
            device_id={"dp": partner(me, order[p])}, device_id_type=MESH,
        )

    def senders(stage):
        return [p for p in range(stages[stage][0], stages[stage][1]) if p != own]

    def reply(p):
        return exchange(backb, homeb, b_send, b_recv, p, p)

    others = [p for p in range(n) if p != own]
    for stage in range(begun):
        for p in senders(stage):
            dispatch(stage, p).start()
    for stage, (low, high, first, end) in enumerate(stages):
        if low <= own < high:
            inbs[stage][own - low] = outb[own, first:end]

    load_outw.wait()
    for lower in range(0, outw.shape[1], LANES):
        outw_t[lower:lower + LANES, :] = outw[:, lower:lower + LANES].T
        gain_t[lower:lower + LANES, :] = jnp.broadcast_to(
            gain_ref[lower // LANES:lower // LANES + 1, :], (LANES, LANES)
        ).T

    row = lax.broadcasted_iota(jnp.int32, (width, width), 0)
    col = lax.broadcasted_iota(jnp.int32, (width, width), 1)
    spread = jnp.where(
        row == jnp.where(col < rows, 2 * col, 2 * (col - rows) + 1), 1.0, 0.0
    ).astype(BF16)
    gathered = jnp.where(
        col == jnp.where(row < rows, 2 * row, 2 * (row - rows) + 1), 1.0, 0.0
    ).astype(BF16)
    low_half = lax.broadcasted_iota(jnp.int32, (rows, LANES), 1) < WIN

    for stage in range(begun, len(stages)):
        for p in senders(stage):
            dispatch(stage, p).start()
    load_qkv.wait()
    for p in senders(0):
        dispatch(0, p).wait()

    def window_in(k, upto):
        at = index_s[CHOSEN, k]
        p, j = at // cap, lax.rem(at, cap)
        found = None
        for (low, high, first, end), landed in zip(stages[:upto], inbs[:upto]):
            part_p = jnp.clip(p, low, high - 1) - low
            part_j = jnp.clip(j, first, end - 1) - first
            value = landed[part_p, part_j].astype(F32)
            if found is None:
                found = value
            else:
                here = (p >= low) & (p < high) & (j >= first) & (j < end)
                found = jnp.where(here, value, found)
        return found

    def unpack(c, upto):
        for p in range(PAIRS):
            first = window_in((c * PAIRS + p) * 2, upto)
            second = window_in((c * PAIRS + p) * 2 + 1, upto)
            even = jnp.where(low_half, first, pltpu.roll(second, WIN, 1))
            odd = jnp.where(low_half, pltpu.roll(first, WIN, 1), second)
            halves = jnp.concatenate([even, odd], axis=0).astype(BF16)
            block = jnp.dot(spread, halves, preferred_element_type=F32).astype(BF16)
            gath[z, c, :, p * LANES:(p + 1) * LANES] = block

    def ag_copy(c, o, step, send):
        return pltpu.make_async_remote_copy(
            src_ref=gath.at[o, c], dst_ref=gath.at[o, c],
            send_sem=send.at[c, o], recv_sem=ag_recv.at[c, o],
            device_id={"mp": z + step}, device_id_type=MESH,
        )

    def ag_own(c):
        @pl.when(z < m - 1)
        def _():
            ag_copy(c, z, 1, ag_right).start()

        @pl.when(z > 0)
        def _():
            ag_copy(c, z, -1, ag_left).start()

    def ag_step(c, t):
        @pl.when(z >= t)
        def _():
            ag_copy(c, z - t, -1, ag_left).wait_recv()

            @pl.when(z < m - 1)
            def _():
                ag_copy(c, z - t, 1, ag_right).start()

        @pl.when(z + t < m)
        def _():
            ag_copy(c, z + t, 1, ag_right).wait_recv()

            @pl.when(z > 0)
            def _():
                ag_copy(c, z + t, -1, ag_left).start()

    def rs_copy(c, s, step, landing, recv):
        return pltpu.make_async_remote_copy(
            src_ref=part.at[c, s], dst_ref=landing.at[c, s],
            send_sem=rs_send.at[c, s], recv_sem=recv.at[c, s],
            device_id={"mp": z + step}, device_id_type=MESH,
        )

    def rs_stage(c, k):
        @pl.when(z == k)
        def _():
            def step(i, _):
                s = m - 1 - i
                if k > 0:
                    rs_copy(c, s, -1, from_left, rs_left).wait_recv()
                    part[c, s] = (part[c, s].astype(F32) + from_left[c, s].astype(F32)).astype(BF16)
                rs_copy(c, s, 1, from_left, rs_left).start()
                return 0

            lax.fori_loop(0, m - 1 - k, step, 0)

        @pl.when(z == m - 1 - k)
        def _():
            def step(s, _):
                if k > 0:
                    rs_copy(c, s, 1, from_right, rs_right).wait_recv()
                    part[c, s] = (part[c, s].astype(F32) + from_right[c, s].astype(F32)).astype(BF16)
                rs_copy(c, s, -1, from_right, rs_right).start()
                return 0

            lax.fori_loop(0, m - 1 - k, step, 0)

    def rs_final(c):
        total[...] = part[c, z].astype(F32)

        @pl.when(z > 0)
        def _():
            rs_copy(c, z, -1, from_left, rs_left).wait_recv()
            total[...] += from_left[c, z].astype(F32)

        @pl.when(z < m - 1)
        def _():
            rs_copy(c, z, 1, from_right, rs_right).wait_recv()
            total[...] += from_right[c, z].astype(F32)

        block = (total[...] + gath[z, c].astype(F32)).astype(BF16)
        halves = jnp.dot(gathered, block, preferred_element_type=F32)
        for p in range(PAIRS):
            even = halves[:rows, p * LANES:(p + 1) * LANES]
            odd = halves[rows:, p * LANES:(p + 1) * LANES]
            k = (c * PAIRS + p) * 2
            done[k] = jnp.where(low_half, even, pltpu.roll(odd, WIN, 1)).astype(BF16)
            done[k + 1] = jnp.where(low_half, pltpu.roll(even, WIN, 1), odd).astype(BF16)

    def project(c):
        full = gath[:, c].reshape(m * width, PAIRS * LANES).astype(F32)
        mean_square = jnp.mean(full * full, axis=0, keepdims=True)
        gain = jnp.concatenate([gain_t[...]] * PAIRS, axis=1)
        normed = (full * lax.rsqrt(mean_square + epsilon) * gain).astype(BF16)
        proj[...] = jnp.dot(qkv_t[...], normed, preferred_element_type=F32).astype(BF16)

    first_window = iota((WIN, LANES), 1) < WIN

    def attend(p):
        lanes = slice(p * LANES, (p + 1) * LANES)
        scores = []
        for h in range(heads_here):
            base = h * 3 * HEAD_DIM
            queries = proj[base:base + HEAD_DIM, lanes]
            key_vecs = proj[base + HEAD_DIM:base + 2 * HEAD_DIM, lanes]
            both = lax.dot_general(
                key_vecs, queries, (((0,), (0,)), ((), ())), preferred_element_type=F32
            )
            scores.append(jnp.where(first_window, both[:WIN], both[WIN:]))
        scores = jnp.concatenate(scores, axis=1) * (HEAD_DIM ** (-0.5) * LOG2E)
        weights = jnp.exp2(scores - jnp.max(scores, axis=0, keepdims=True))
        probs = weights * (1.0 / jnp.sum(weights, axis=0, keepdims=True))
        for h in range(heads_here):
            base = h * 3 * HEAD_DIM
            value_vecs = proj[base + 2 * HEAD_DIM:base + 3 * HEAD_DIM, lanes]
            mine = probs[:, h * LANES:(h + 1) * LANES]
            spread_probs = jnp.concatenate(
                [jnp.where(first_window, mine, 0.0), jnp.where(first_window, 0.0, mine)], axis=0
            ).astype(BF16)
            heads[h * HEAD_DIM:(h + 1) * HEAD_DIM, lanes] = jnp.dot(
                value_vecs, spread_probs, preferred_element_type=F32
            ).astype(BF16)

    def output(c):
        for s in range(m):
            part[c, s] = jnp.dot(
                outw_t[s * width:(s + 1) * width, :], heads[...], preferred_element_type=F32
            ).astype(BF16)

    chunk_win = 2 * PAIRS
    needed = [stages_needed(n, cap, c) for c in range(chunks)]

    def own_chunk(c):
        for stage in range(1, len(stages)):
            @pl.when(c == sum(upto <= stage for upto in needed))
            def _():
                for p in senders(stage):
                    dispatch(stage, p).wait()

        for upto in sorted(set(needed)):
            low = needed.index(upto)

            @pl.when(jnp.logical_and(c >= low, c < low + needed.count(upto)))
            def _():
                unpack(c, upto)

        ag_own(c)

    def ready(p):
        return (min(ENC_WIN, cap * (p + 1)) - 1) // chunk_win

    def answer(p):
        for j in range(cap):
            backb[p, j] = done[index_s[BACK, p * cap + j]]
        if p != own:
            reply(p).start()

    def finish(c):
        rs_final(c)
        for p in range(n):
            if ready(p) < chunks - 1:
                pl.when(c == ready(p))(functools.partial(answer, p))


    def within(c, act):
        @pl.when(jnp.logical_and(c >= 0, c < chunks))
        def _():
            act(c)

    def compute(c):
        project(c)
        for p in range(PAIRS):
            attend(p)
        output(c)

    def turn(i, _):
        c = i - (m - 1)
        for t in range(m - 1, 0, -1):
            within(c + m - 1 - t, lambda at, t=t: ag_step(at, t))
        within(c + m - 1, own_chunk)
        within(c, compute)
        within(c, lambda at: rs_stage(at, 0))
        for k in range(1, m - 1):
            within(c - k, lambda at, k=k: rs_stage(at, k))
        within(c - (m - 1), finish)
        return 0

    lax.fori_loop(0, chunks + 2 * (m - 1), turn, 0)

    for p in range(n):
        if ready(p) == chunks - 1:
            answer(p)
    homeb[own] = backb[own]
    homeb[n] = jnp.zeros_like(homeb[n])

    def sent(c, _):
        def each(o, _):
            @pl.when(jnp.logical_and(z < m - 1, o <= z))
            def _():
                ag_copy(c, o, 1, ag_right).wait_send()

            @pl.when(jnp.logical_and(z > 0, o >= z))
            def _():
                ag_copy(c, o, -1, ag_left).wait_send()

            @pl.when(o > z)
            def _():
                rs_copy(c, o, 1, from_left, rs_left).wait_send()

            @pl.when(o < z)
            def _():
                rs_copy(c, o, -1, from_right, rs_right).wait_send()

            return 0

        return lax.fori_loop(0, m, each, 0)

    lax.fori_loop(0, chunks, sent, 0)
    for p in others:
        reply(p).wait()

    home_ref[...] = homeb[...]
    slots_ref[...] = index_v[...]


def place_kernel(slots_ref, home_ref, out_ref, flat):
    groups, rows = out_ref.shape[:2]
    cap = home_ref.shape[1]

    def place_home(s, _):
        at = slots_ref[SLOT, s]
        flat[window_rows(s, rows), :] = home_ref[at // cap, lax.rem(at, cap)].astype(F32)
        return 0

    lax.fori_loop(0, groups * TILE, place_home, 0)

    def narrow(g, _):
        at = pl.ds(pl.multiple_of(g * (rows * TILE), rows * TILE), rows * TILE)
        out_ref[g] = flat[at, :].astype(BF16).reshape(rows, TILE, LANES)
        return 0

    lax.fori_loop(0, groups, narrow, 0)


def body(patches, norm_gain, qkv_weight, out_weight, window_plan):
    n = lax.axis_size("dp")
    m = lax.axis_size("mp")
    home_win, row_width = patches.shape
    rows = row_width // LANES
    width = 2 * rows
    full_width = width * m
    cap = (home_win + n - 1) // n
    chunks = ENC_WIN // (2 * PAIRS)
    cols = PAIRS * LANES
    stages = arrival_stages(n, cap)

    tiles = jnp.transpose(
        patches.reshape(home_win // TILE, TILE, rows, LANES), (0, 2, 1, 3)
    )
    hbm = pl.BlockSpec(memory_space=pl.ANY)
    vmem = pl.BlockSpec(memory_space=pltpu.VMEM)
    dma = pltpu.SemaphoreType.DMA
    answers, index = pl.pallas_call(
        functools.partial(kernel, n, m, cap),
        out_shape=[
            jax.ShapeDtypeStruct((n + 1, cap, rows, LANES), BF16),
            jax.ShapeDtypeStruct((8, LANES), jnp.int32),
        ],
        in_specs=[vmem] * 3 + [hbm] * 2,
        out_specs=[vmem, vmem],
        scratch_shapes=[
            pltpu.VMEM((8, LANES), jnp.int32),
            pltpu.SMEM((8, LANES), jnp.int32),
            pltpu.VMEM((home_win * rows, LANES), F32),
            pltpu.VMEM(out_weight.shape, BF16),
            pltpu.VMEM((full_width, LANES), F32),
            pltpu.VMEM((n, cap, rows, LANES), BF16),
            [
                pltpu.VMEM((high - low, end - first, rows, LANES), BF16)
                for low, high, first, end in stages
            ],
            pltpu.VMEM((m, chunks, width, cols), BF16),
            pltpu.VMEM((qkv_weight.shape[1], full_width), BF16),
            pltpu.VMEM((full_width, out_weight.shape[0]), BF16),
            pltpu.VMEM((qkv_weight.shape[1], cols), BF16),
            pltpu.VMEM((out_weight.shape[0], cols), BF16),
            pltpu.VMEM((chunks, m, width, cols), BF16),
            pltpu.VMEM((chunks, m, width, cols), BF16),
            pltpu.VMEM((chunks, m, width, cols), BF16),
            pltpu.VMEM((width, cols), F32),
            pltpu.VMEM((ENC_WIN, rows, LANES), BF16),
            pltpu.VMEM((n, cap, rows, LANES), BF16),
            pltpu.VMEM((n + 1, cap, rows, LANES), BF16),
            dma, dma((2,)), dma((len(stages), n)), dma((len(stages), n)), dma((n,)), dma((n,)),
            dma((chunks, m)), dma((chunks, m)), dma((chunks, m)),
            dma((chunks, m)), dma((chunks, m)), dma((chunks, m)),
        ],
        compiler_params=pltpu.CompilerParams(
            collective_id=0, has_side_effects=True, vmem_limit_bytes=56 * 1024 * 1024
        ),
    )(
        window_plan, tiles, norm_gain.reshape(-1, LANES),
        qkv_weight.T, out_weight,
    )
    result = pl.pallas_call(
        place_kernel,
        out_shape=jax.ShapeDtypeStruct(tiles.shape, BF16),
        in_specs=[pl.BlockSpec(memory_space=pltpu.SMEM), vmem],
        out_specs=vmem,
        scratch_shapes=[pltpu.VMEM((home_win * rows, LANES), F32)],
        compiler_params=pltpu.CompilerParams(vmem_limit_bytes=24 * 1024 * 1024),
    )(index, answers)
    return jnp.transpose(result, (0, 2, 1, 3)).reshape(home_win, row_width)


def solution(mesh):
    return jax.shard_map(
        body,
        mesh=mesh,
        in_specs=(P("dp", "mp"), P(), P(None, "mp"), P("mp", None), P()),
        out_specs=P("dp", "mp"),
        check_vma=False,
    )
```

```python
import functools

import jax
import jax.numpy as jnp
from jax import lax
from jax.experimental import pallas as pl
from jax.experimental.pallas import tpu as pltpu
from jax.sharding import PartitionSpec as P

HEAD_DIM = 80
WIN = 64
ENC_WIN = 16
LANES = 128
PAIRS = 1
TILE = 8

LOG2E = 1.4426950408889634
epsilon = 1e-06
MESH = pl.DeviceIdType.MESH
F32 = jnp.float32
BF16 = jnp.bfloat16


SOURCE, CHOSEN, BACK, SLOT = range(4)


def early_positions(n, cap):
    return n - (ENC_WIN - 2 * PAIRS) // cap


def arrival_stages(n, cap):
    early, reach = early_positions(n, cap), min(cap, 2 * PAIRS)
    stages = [(0, early, 0, reach), (0, early, reach, cap)]
    stages += [(early, early + 1, 0, cap), (early + 1, n, 0, cap)]
    return [part for part in stages if part[0] < part[1] and part[2] < part[3]]


def early_stages(n, cap):
    return sum(part[0] == 0 for part in arrival_stages(n, cap))


def stages_needed(n, cap, c):
    last = (c + 1) * 2 * PAIRS - 1
    positions = n - (ENC_WIN - 1 - last) // cap
    return max(
        at + 1
        for at, (low, _, first, _) in enumerate(arrival_stages(n, cap))
        if low < positions and first <= last
    )


def position_order(n, cap):
    far = list(range(n - 2, 1, -2)) + list(range(n - 1, 2, -2))
    split = early_positions(n, cap) - 2
    return far[:split] + [1, 0] + far[split:]


def position_of(flip, n, cap):
    split = early_positions(n, cap) - 2
    at = jnp.where(flip % 2 == 0, (n - 2 - flip) // 2, n // 2 - 1 + (n - 1 - flip) // 2)
    at = jnp.where(at >= split, at + 2, at)
    return jnp.where(flip == 1, split, jnp.where(flip == 0, split + 1, at))


def partner(me, flip):
    other, bit = me, 1
    while bit <= flip:
        if (flip // bit) % 2:
            other = other + bit * (1 - 2 * ((me // bit) % 2))
        bit *= 2
    return other


def iota(shape, axis):
    return lax.broadcasted_iota(jnp.int32, shape, axis)


def plan_indices(n, cap, me, plan_ref, index_v):
    plan = plan_ref[...]
    index_v[...] = jnp.zeros_like(index_v)
    slots = plan.shape[1]
    mine = plan_ref[pl.ds(me, 1), :]
    same = iota((slots, slots), 0) == iota((slots, slots), 1)
    turned = jnp.sum(jnp.where(same, mine, 0), axis=1, keepdims=True)
    earlier = (turned == mine) & (iota((slots, slots), 1) < iota((slots, slots), 0))
    ordinal = jnp.sum(earlier.astype(jnp.int32), axis=1, keepdims=True)
    place = jnp.where(turned >= 0, position_of(turned ^ me, n, cap) * cap + ordinal, n * cap)
    grid = (slots, n * cap)
    source = jnp.sum(
        jnp.where(place == iota(grid, 1), iota(grid, 0), 0), axis=0, keepdims=True
    )
    index_v[SOURCE:SOURCE + 1, :n * cap] = jnp.clip(source, 0, slots - 1)
    index_v[SLOT:SLOT + 1, :slots] = jnp.minimum(
        jnp.sum(jnp.where(same, place, 0), axis=0, keepdims=True), n * cap
    )

    counts = jnp.sum((plan == me).astype(jnp.int32), axis=1, keepdims=True)
    square = (n, n)
    counts_row = jnp.sum(
        jnp.where(iota(square, 0) == iota(square, 1), counts, 0), axis=0, keepdims=True
    )
    at_col = position_of(iota((n, 1), 0) ^ me, n, cap)
    at_row = position_of(iota((1, n), 1) ^ me, n, cap)
    offsets = jnp.sum(jnp.where(at_row < at_col, counts_row, 0), axis=1, keepdims=True)
    j = iota((n, ENC_WIN), 1) - offsets
    chosen = jnp.sum(
        jnp.where((j >= 0) & (j < counts), at_col * cap + j, 0), axis=0, keepdims=True
    )
    index_v[CHOSEN:CHOSEN + 1, :ENC_WIN] = jnp.clip(chosen, 0, n * cap - 1)
    q = iota((n, n * cap), 1)
    back = jnp.sum(
        jnp.where(q // cap == at_col, offsets + q % cap, 0), axis=0, keepdims=True
    )
    index_v[BACK:BACK + 1, :n * cap] = jnp.clip(back, 0, ENC_WIN - 1)


def kernel(
    n, m, cap,
    plan_ref, x_ref, gain_ref, qkv_ref, outw_ref,
    out_ref,
    index_v, index_s, flat, outw, gain_t, outb, inbs, gath, qkv_t, outw_t, proj, heads, part, from_left, from_right, total, done, backb, homeb,
    i_sem, w_sem, d_send, d_recv, b_send, b_recv, ag_recv, ag_right, ag_left, rs_send, rs_left, rs_right,
):
    me = lax.axis_index("dp")
    z = lax.axis_index("mp")
    rows = x_ref.shape[1]
    home_win = x_ref.shape[0] * TILE
    width = 2 * rows
    chunks = gath.shape[1]
    heads_here = qkv_ref.shape[0] // (3 * HEAD_DIM)

    order = position_order(n, cap)

    load_qkv = pltpu.make_async_copy(qkv_ref, qkv_t, w_sem.at[0])
    load_outw = pltpu.make_async_copy(outw_ref, outw, w_sem.at[1])
    load_qkv.start()
    load_outw.start()

    barrier = pltpu.get_barrier_semaphore()

    for d in range(1, n):
        pl.semaphore_signal(
            barrier, inc=1, device_id={"dp": partner(me, d)}, device_id_type=MESH
        )

    @pl.when(z > 0)
    def _():
        pl.semaphore_signal(barrier, inc=1, device_id={"mp": z - 1}, device_id_type=MESH)

    @pl.when(z < m - 1)
    def _():
        pl.semaphore_signal(barrier, inc=1, device_id={"mp": z + 1}, device_id_type=MESH)

    plan_indices(n, cap, me, plan_ref, index_v)
    load_index = pltpu.make_async_copy(index_v, index_s, i_sem)
    load_index.start()

    def widen(g, _):
        at = pl.ds(pl.multiple_of(g * (rows * TILE), rows * TILE), rows * TILE)
        flat[at, :] = x_ref[g].reshape(rows * TILE, LANES).astype(F32)
        return 0

    lax.fori_loop(0, home_win // TILE, widen, 0)
    load_index.wait()

    def window_rows(s):
        return pl.ds((s // TILE) * (rows * TILE) + lax.rem(s, TILE), rows, stride=TILE)

    for p in range(n):
        for j in range(cap):
            outb[p, j] = flat[window_rows(index_s[SOURCE, p * cap + j]), :].astype(BF16)

    ends = (z == 0).astype(jnp.int32) + (z == m - 1).astype(jnp.int32)
    pl.semaphore_wait(barrier, n + 1 - ends)

    own = order.index(0)

    own = order.index(0)
    stages = arrival_stages(n, cap)
    begun = early_stages(n, cap)

    def exchange(src, dst, send, recv, p, at):
        return pltpu.make_async_remote_copy(
            src_ref=src.at[p], dst_ref=dst.at[at], send_sem=send.at[p], recv_sem=recv.at[p],
            device_id={"dp": partner(me, order[p])}, device_id_type=MESH,
        )

    def dispatch(stage, p):
        low, _, first, end = stages[stage]
        return pltpu.make_async_remote_copy(
            src_ref=outb.at[p, pl.ds(first, end - first)], dst_ref=inbs[stage].at[p - low],
            send_sem=d_send.at[stage, p], recv_sem=d_recv.at[stage, p],
            device_id={"dp": partner(me, order[p])}, device_id_type=MESH,
        )

    def senders(stage):
        return [p for p in range(stages[stage][0], stages[stage][1]) if p != own]

    def reply(p):
        return exchange(backb, homeb, b_send, b_recv, p, p)

    others = [p for p in range(n) if p != own]
    for stage in range(begun):
        for p in senders(stage):
            dispatch(stage, p).start()
    for stage, (low, high, first, end) in enumerate(stages):
        if low <= own < high:
            inbs[stage][own - low] = outb[own, first:end]

    load_outw.wait()
    for lower in range(0, outw.shape[1], LANES):
        outw_t[lower:lower + LANES, :] = outw[:, lower:lower + LANES].T
        gain_t[lower:lower + LANES, :] = jnp.broadcast_to(
            gain_ref[lower // LANES:lower // LANES + 1, :], (LANES, LANES)
        ).T

    row = lax.broadcasted_iota(jnp.int32, (width, width), 0)
    col = lax.broadcasted_iota(jnp.int32, (width, width), 1)
    spread = jnp.where(
        row == jnp.where(col < rows, 2 * col, 2 * (col - rows) + 1), 1.0, 0.0
    ).astype(BF16)
    gathered = jnp.where(
        col == jnp.where(row < rows, 2 * row, 2 * (row - rows) + 1), 1.0, 0.0
    ).astype(BF16)
    low_half = lax.broadcasted_iota(jnp.int32, (rows, LANES), 1) < WIN

    for stage in range(begun, len(stages)):
        for p in senders(stage):
            dispatch(stage, p).start()
    load_qkv.wait()
    for p in senders(0):
        dispatch(0, p).wait()

    def window_in(k, upto):
        at = index_s[CHOSEN, k]
        p, j = at // cap, lax.rem(at, cap)
        found = None
        for (low, high, first, end), landed in zip(stages[:upto], inbs[:upto]):
            part_p = jnp.clip(p, low, high - 1) - low
            part_j = jnp.clip(j, first, end - 1) - first
            value = landed[part_p, part_j].astype(F32)
            if found is None:
                found = value
            else:
                here = (p >= low) & (p < high) & (j >= first) & (j < end)
                found = jnp.where(here, value, found)
        return found

    def unpack(c, upto):
        for p in range(PAIRS):
            first = window_in((c * PAIRS + p) * 2, upto)
            second = window_in((c * PAIRS + p) * 2 + 1, upto)
            even = jnp.where(low_half, first, pltpu.roll(second, WIN, 1))
            odd = jnp.where(low_half, pltpu.roll(first, WIN, 1), second)
            halves = jnp.concatenate([even, odd], axis=0).astype(BF16)
            block = jnp.dot(spread, halves, preferred_element_type=F32).astype(BF16)
            gath[z, c, :, p * LANES:(p + 1) * LANES] = block

    def ag_copy(c, o, step, send):
        return pltpu.make_async_remote_copy(
            src_ref=gath.at[o, c], dst_ref=gath.at[o, c],
            send_sem=send.at[c, o], recv_sem=ag_recv.at[c, o],
            device_id={"mp": z + step}, device_id_type=MESH,
        )

    def ag_own(c):
        @pl.when(z < m - 1)
        def _():
            ag_copy(c, z, 1, ag_right).start()

        @pl.when(z > 0)
        def _():
            ag_copy(c, z, -1, ag_left).start()

    def ag_step(c, t):
        @pl.when(z >= t)
        def _():
            ag_copy(c, z - t, -1, ag_left).wait_recv()

            @pl.when(z < m - 1)
            def _():
                ag_copy(c, z - t, 1, ag_right).start()

        @pl.when(z + t < m)
        def _():
            ag_copy(c, z + t, 1, ag_right).wait_recv()

            @pl.when(z > 0)
            def _():
                ag_copy(c, z + t, -1, ag_left).start()

    def rs_copy(c, s, step, landing, recv):
        return pltpu.make_async_remote_copy(
            src_ref=part.at[c, s], dst_ref=landing.at[c, s],
            send_sem=rs_send.at[c, s], recv_sem=recv.at[c, s],
            device_id={"mp": z + step}, device_id_type=MESH,
        )

    def rs_stage(c, k):
        @pl.when(z == k)
        def _():
            def step(i, _):
                s = m - 1 - i
                if k > 0:
                    rs_copy(c, s, -1, from_left, rs_left).wait_recv()
                    part[c, s] = (part[c, s].astype(F32) + from_left[c, s].astype(F32)).astype(BF16)
                rs_copy(c, s, 1, from_left, rs_left).start()
                return 0

            lax.fori_loop(0, m - 1 - k, step, 0)

        @pl.when(z == m - 1 - k)
        def _():
            def step(s, _):
                if k > 0:
                    rs_copy(c, s, 1, from_right, rs_right).wait_recv()
                    part[c, s] = (part[c, s].astype(F32) + from_right[c, s].astype(F32)).astype(BF16)
                rs_copy(c, s, -1, from_right, rs_right).start()
                return 0

            lax.fori_loop(0, m - 1 - k, step, 0)

    def rs_final(c):
        total[...] = part[c, z].astype(F32)

        @pl.when(z > 0)
        def _():
            rs_copy(c, z, -1, from_left, rs_left).wait_recv()
            total[...] += from_left[c, z].astype(F32)

        @pl.when(z < m - 1)
        def _():
            rs_copy(c, z, 1, from_right, rs_right).wait_recv()
            total[...] += from_right[c, z].astype(F32)

        block = (total[...] + gath[z, c].astype(F32)).astype(BF16)
        halves = jnp.dot(gathered, block, preferred_element_type=F32)
        for p in range(PAIRS):
            even = halves[:rows, p * LANES:(p + 1) * LANES]
            odd = halves[rows:, p * LANES:(p + 1) * LANES]
            k = (c * PAIRS + p) * 2
            done[k] = jnp.where(low_half, even, pltpu.roll(odd, WIN, 1)).astype(BF16)
            done[k + 1] = jnp.where(low_half, pltpu.roll(even, WIN, 1), odd).astype(BF16)

    def project(c):
        full = gath[:, c].reshape(m * width, PAIRS * LANES).astype(F32)
        mean_square = jnp.mean(full * full, axis=0, keepdims=True)
        gain = jnp.concatenate([gain_t[...]] * PAIRS, axis=1)
        normed = (full * lax.rsqrt(mean_square + epsilon) * gain).astype(BF16)
        proj[...] = jnp.dot(qkv_t[...], normed, preferred_element_type=F32).astype(BF16)

    first_window = iota((WIN, LANES), 1) < WIN

    def attend(p):
        lanes = slice(p * LANES, (p + 1) * LANES)
        scores = []
        for h in range(heads_here):
            base = h * 3 * HEAD_DIM
            queries = proj[base:base + HEAD_DIM, lanes]
            key_vecs = proj[base + HEAD_DIM:base + 2 * HEAD_DIM, lanes]
            both = lax.dot_general(
                key_vecs, queries, (((0,), (0,)), ((), ())), preferred_element_type=F32
            )
            scores.append(jnp.where(first_window, both[:WIN], both[WIN:]))
        scores = jnp.concatenate(scores, axis=1) * (HEAD_DIM ** (-0.5) * LOG2E)
        weights = jnp.exp2(scores - jnp.max(scores, axis=0, keepdims=True))
        probs = weights * (1.0 / jnp.sum(weights, axis=0, keepdims=True))
        for h in range(heads_here):
            base = h * 3 * HEAD_DIM
            value_vecs = proj[base + 2 * HEAD_DIM:base + 3 * HEAD_DIM, lanes]
            mine = probs[:, h * LANES:(h + 1) * LANES]
            spread_probs = jnp.concatenate(
                [jnp.where(first_window, mine, 0.0), jnp.where(first_window, 0.0, mine)], axis=0
            ).astype(BF16)
            heads[h * HEAD_DIM:(h + 1) * HEAD_DIM, lanes] = jnp.dot(
                value_vecs, spread_probs, preferred_element_type=F32
            ).astype(BF16)

    def output(c):
        for s in range(m):
            part[c, s] = jnp.dot(
                outw_t[s * width:(s + 1) * width, :], heads[...], preferred_element_type=F32
            ).astype(BF16)

    chunk_win = 2 * PAIRS
    needed = [stages_needed(n, cap, c) for c in range(chunks)]

    def own_chunk(c):
        for stage in range(1, len(stages)):
            @pl.when(c == sum(upto <= stage for upto in needed))
            def _():
                for p in senders(stage):
                    dispatch(stage, p).wait()

        for upto in sorted(set(needed)):
            low = needed.index(upto)

            @pl.when(jnp.logical_and(c >= low, c < low + needed.count(upto)))
            def _():
                unpack(c, upto)

        ag_own(c)

    def ready(p):
        return (min(ENC_WIN, cap * (p + 1)) - 1) // chunk_win

    def answer(p):
        for j in range(cap):
            backb[p, j] = done[index_s[BACK, p * cap + j]]
        if p != own:
            reply(p).start()

    def finish(c):
        rs_final(c)
        for p in range(n):
            if ready(p) < chunks - 1:
                pl.when(c == ready(p))(functools.partial(answer, p))


    def within(c, act):
        @pl.when(jnp.logical_and(c >= 0, c < chunks))
        def _():
            act(c)

    def compute(c):
        project(c)
        for p in range(PAIRS):
            attend(p)
        output(c)

    def turn(i, _):
        c = i - (m - 1)
        for t in range(m - 1, 0, -1):
            within(c + m - 1 - t, lambda at, t=t: ag_step(at, t))
        within(c + m - 1, own_chunk)
        within(c, compute)
        for k in range(m - 2, -1, -1):
            within(c - k, lambda at, k=k: rs_stage(at, k))
        within(c - (m - 1), finish)
        return 0

    lax.fori_loop(0, chunks + 2 * (m - 1), turn, 0)

    for p in range(n):
        if ready(p) == chunks - 1:
            answer(p)
    homeb[own] = backb[own]
    homeb[n] = jnp.zeros_like(homeb[n])

    def sent(c, _):
        def each(o, _):
            @pl.when(jnp.logical_and(z < m - 1, o <= z))
            def _():
                ag_copy(c, o, 1, ag_right).wait_send()

            @pl.when(jnp.logical_and(z > 0, o >= z))
            def _():
                ag_copy(c, o, -1, ag_left).wait_send()

            @pl.when(o > z)
            def _():
                rs_copy(c, o, 1, from_left, rs_left).wait_send()

            @pl.when(o < z)
            def _():
                rs_copy(c, o, -1, from_right, rs_right).wait_send()

            return 0

        return lax.fori_loop(0, m, each, 0)

    lax.fori_loop(0, chunks, sent, 0)
    for p in others:
        reply(p).wait()

    def place_home(s, _):
        at = index_s[SLOT, s]
        flat[window_rows(s), :] = homeb[at // cap, lax.rem(at, cap)].astype(F32)
        return 0

    lax.fori_loop(0, home_win, place_home, 0)

    def narrow(g, _):
        at = pl.ds(pl.multiple_of(g * (rows * TILE), rows * TILE), rows * TILE)
        out_ref[g] = flat[at, :].astype(BF16).reshape(rows, TILE, LANES)
        return 0

    lax.fori_loop(0, home_win // TILE, narrow, 0)


def body(patches, norm_gain, qkv_weight, out_weight, window_plan):
    n = lax.axis_size("dp")
    m = lax.axis_size("mp")
    home_win, row_width = patches.shape
    rows = row_width // LANES
    width = 2 * rows
    full_width = width * m
    cap = (home_win + n - 1) // n
    chunks = ENC_WIN // (2 * PAIRS)
    cols = PAIRS * LANES
    stages = arrival_stages(n, cap)

    tiles = jnp.transpose(
        patches.reshape(home_win // TILE, TILE, rows, LANES), (0, 2, 1, 3)
    )
    hbm = pl.BlockSpec(memory_space=pl.ANY)
    vmem = pl.BlockSpec(memory_space=pltpu.VMEM)
    dma = pltpu.SemaphoreType.DMA
    result = pl.pallas_call(
        functools.partial(kernel, n, m, cap),
        out_shape=jax.ShapeDtypeStruct(tiles.shape, BF16),
        in_specs=[vmem] * 3 + [hbm] * 2,
        out_specs=vmem,
        scratch_shapes=[
            pltpu.VMEM((8, LANES), jnp.int32),
            pltpu.SMEM((8, LANES), jnp.int32),
            pltpu.VMEM((home_win * rows, LANES), F32),
            pltpu.VMEM(out_weight.shape, BF16),
            pltpu.VMEM((full_width, LANES), F32),
            pltpu.VMEM((n, cap, rows, LANES), BF16),
            [
                pltpu.VMEM((high - low, end - first, rows, LANES), BF16)
                for low, high, first, end in stages
            ],
            pltpu.VMEM((m, chunks, width, cols), BF16),
            pltpu.VMEM((qkv_weight.shape[1], full_width), BF16),
            pltpu.VMEM((full_width, out_weight.shape[0]), BF16),
            pltpu.VMEM((qkv_weight.shape[1], cols), BF16),
            pltpu.VMEM((out_weight.shape[0], cols), BF16),
            pltpu.VMEM((chunks, m, width, cols), BF16),
            pltpu.VMEM((chunks, m, width, cols), BF16),
            pltpu.VMEM((chunks, m, width, cols), BF16),
            pltpu.VMEM((width, cols), F32),
            pltpu.VMEM((ENC_WIN, rows, LANES), BF16),
            pltpu.VMEM((n, cap, rows, LANES), BF16),
            pltpu.VMEM((n + 1, cap, rows, LANES), BF16),
            dma, dma((2,)), dma((len(stages), n)), dma((len(stages), n)), dma((n,)), dma((n,)),
            dma((chunks, m)), dma((chunks, m)), dma((chunks, m)),
            dma((chunks, m)), dma((chunks, m)), dma((chunks, m)),
        ],
        compiler_params=pltpu.CompilerParams(
            collective_id=0, has_side_effects=True, vmem_limit_bytes=56 * 1024 * 1024
        ),
    )(
        window_plan, tiles, norm_gain.reshape(-1, LANES),
        qkv_weight.T, out_weight,
    )
    return jnp.transpose(result, (0, 2, 1, 3)).reshape(home_win, row_width)


def solution(mesh):
    return jax.shard_map(
        body,
        mesh=mesh,
        in_specs=(P("dp", "mp"), P(), P(None, "mp"), P("mp", None), P()),
        out_specs=P("dp", "mp"),
        check_vma=False,
    )
```
